128 devices in a mesh: grp: 8 (over x, y_hi), dp: 16 (over z, y_lo, core).
Axes of the slice: x: 4, y: 4 (y_hi: 2, y_lo: 2; y = y_hi * 2 + y_lo), z: 4, core: 2. Of those that a mesh axis runs over, the one named last changes fastest.
Arguments:
- queries: bfloat16 [16, 2048, 1280], P('dp', 'grp'), may hold values from -8 to 8
- keys_in: bfloat16 [16, 2048, 1280], P('dp', 'grp'), may hold values from -8 to 8
- value_rows: bfloat16 [16, 2048, 1280], P('dp', 'grp'), may hold values from -6 to 6
- grad_out: bfloat16 [16, 2048, 1280], P('dp', 'grp'), may hold values from -6 to 6
- out_weight: bfloat16 [1280, 1280], replicated, may hold values from -0.15625 to 0.15625
- image_ids: int32 [16, 16], P('dp'), may hold values from 0 to 3, never falling along the last dimension, each value on 1 to 12 neighbouring positions
Outputs:
- grad_queries: bfloat16 [16, 2048, 1280], P('dp', 'grp')
- grad_keys: bfloat16 [16, 2048, 1280], P('dp', 'grp')
- grad_values: bfloat16 [16, 2048, 1280], P('dp', 'grp')
- grad_weight: float32 [1280, 1280], replicated
The draws below stay inside these ranges and needn't reach their ends.
Inputs may be any that keep to these rules, and one draw needn't show every extreme that they name: `image_ids`: image numbers never fall along a sequence; each sequence holds 4 images of 1 to 12 blocks, one of exactly that many.
All inputs are finite; a program needn't handle non-finite values.
Results may differ from the reference program's by a relative error of at most 0.011.
Values may be sent and summed in bfloat16 or wider, within the bound.
No kernel may reach another device: no remote copies, remote signals or barrier semaphores. Data moves between devices by JAX's collectives and lax.ppermute only.
A program may use at most 128 MiB of HBM per device.

```python
import math
import jax
import jax.numpy as jnp
import numpy as np
from jax import lax

HEADS = 16
BLK = 128
D = 1280
GBLOCKS = 16
SEQ = 2048
TOKENS = 32768
N_DP = 16


def draw_queries(key, part):
    key = jax.random.fold_in(key, 11)
    result = jnp.clip(jax.random.normal(key, (N_DP, SEQ, D), jnp.float32), -8.0, 8.0)
    return result.astype(jnp.bfloat16)


def draw_keys_in(key, part):
    key = jax.random.fold_in(key, 23)
    result = jnp.clip(jax.random.normal(key, (N_DP, SEQ, D), jnp.float32), -8.0, 8.0)
    return result.astype(jnp.bfloat16)


def level_of(key, extent, split, low, largest):
    factor_of = 1.0
    for axis_at, shards_of in split:
        steps = jax.random.uniform(jax.random.fold_in(jax.random.fold_in(key, 6), axis_at), (shards_of,), jnp.float32, low / len(split), largest / len(split))
        factor_of = factor_of * jnp.repeat(jnp.exp(steps), extent[axis_at] // shards_of).reshape((-1,) + (1,) * (len(extent) - 1 - axis_at))
    return factor_of


def split_up(count, total, reach, lean):
    loads = [(1 << 20) // math.isqrt(grade ** lean) + 1 for grade in range(2, count + 1)]
    rest, holding = total - reach - (count - 1), [1] * (count - 1)
    while rest > 0:
        movable = [i for i in range(count - 1) if holding[i] < reach]
        whole, remaining = sum([loads[i] for i in movable]), rest
        for i in movable:
            extra = min(reach - holding[i], max(1, remaining * loads[i] // whole), rest)
            holding[i] = holding[i] + extra
            rest = rest - extra
    return np.array([reach] + holding)


def ragged_sizes(own_key, number_of, total, reach, lean):
    if number_of == 2:
        one = jax.random.randint(own_key, (), max(1, total - reach), min(reach, total - 1) + 1)
        return jnp.stack([one, total - one])
    sizes = jnp.asarray(split_up(number_of, total, reach, lean), jnp.int32)
    pairs = (number_of - 1) // 2
    donor, taker = sizes[1:1 + 2 * pairs:2], sizes[2:2 + 2 * pairs:2]
    margin = jnp.minimum(donor - 1, reach - taker)
    moved = jax.random.randint(jax.random.fold_in(own_key, 1), (pairs,), 0, 1 << 20) % (margin + 1)
    sizes = sizes.at[1:1 + 2 * pairs:2].set(donor - moved).at[2:2 + 2 * pairs:2].set(taker + moved)
    return sizes[jax.random.permutation(jax.random.fold_in(own_key, 2), number_of)]


def normal_values(stream_key, extent, spread, limit, shards=(), kind=jnp.bfloat16):
    values = spread * jax.random.normal(stream_key, extent, jnp.float32)
    if shards:
        values = values * level_of(stream_key, extent, shards, -0.22, 0.18)
    return jnp.clip(values, -limit, limit).astype(kind)


def setup_inputs(seed: int = 0) -> dict:
    key_list = jax.random.split(jax.random.key(seed), 7)
    return {
        "queries": draw_queries(jax.random.fold_in(key_list[6], 71), 0),
        "keys_in": draw_keys_in(jax.random.fold_in(key_list[6], 71), 0),
        "value_rows": normal_values(key_list[2], (N_DP, SEQ, D), 1.0, 6.0, ((0, 16), (1, 8))),
        "grad_out": normal_values(key_list[3], (N_DP, SEQ, D), 1.0, 6.0, ((0, 16), (1, 8))),
        "out_weight": normal_values(key_list[4], (D, D), D ** -0.5, 0.15625),
        "image_ids": jax.vmap(lambda own: jnp.searchsorted(jnp.cumsum(ragged_sizes(own, GBLOCKS // 4, GBLOCKS, GBLOCKS - GBLOCKS // 4, 2)), jnp.arange(GBLOCKS), side="right"))(jax.random.split(key_list[5], N_DP)).reshape((N_DP, GBLOCKS)).astype(jnp.int32),
    }


def inner(left, right):
    return lax.dot_general(left, right, (((1,), (1,)), ((), ())), preferred_element_type=jnp.float32)

def outer(left, right):
    return lax.dot_general(left, right, (((0,), (0,)), ((), ())), preferred_element_type=jnp.float32)

def head_grads(query_h, key_h, value_h, attn_h, query_ids, key_ids):
    scaling = 1.0 / math.sqrt(query_h.shape[-1])
    scores = inner(query_h, key_h) * scaling
    same_image = query_ids[:, None] == key_ids[None, :]
    masked = jnp.where(same_image, scores, -1e+30)
    row_max = lax.optimization_barrier(jnp.max(masked, axis=1, keepdims=True))
    weights_raw = jnp.where(same_image, jnp.exp(masked - row_max), 0.0)
    probs = weights_raw / lax.optimization_barrier(jnp.sum(weights_raw, axis=1, keepdims=True))
    probs_low = probs.astype(jnp.bfloat16)
    attended = jnp.dot(probs_low, value_h, preferred_element_type=jnp.float32).astype(jnp.bfloat16)
    deltas = lax.optimization_barrier(jnp.sum(attn_h.astype(jnp.float32) * attended.astype(jnp.float32), axis=1, keepdims=True))
    dprobs = inner(attn_h, value_h)
    dscores = (probs * (dprobs - deltas)).astype(jnp.bfloat16)
    grad_query = jnp.dot(dscores, key_h, preferred_element_type=jnp.float32) * scaling
    grad_key = outer(dscores, query_h) * scaling
    grad_value = outer(probs_low, attn_h)
    return (attended, grad_query, grad_key, grad_value)

def all_heads(query_r, key_r, value_r, attn_r, query_ids, key_ids, heads):

    def split_heads(array):
        return array.reshape(array.shape[0], heads, -1).transpose(1, 0, 2)

    def join_heads(array):
        return array.transpose(1, 0, 2).reshape(array.shape[1], -1)

    def per_head(parts):
        return head_grads(parts[0], parts[1], parts[2], parts[3], query_ids, key_ids)
    results = lax.map(per_head, (split_heads(query_r), split_heads(key_r), split_heads(value_r), split_heads(attn_r)))
    return tuple((join_heads(item) for item in results))

def reference(queries, keys_in, value_rows, grad_out, out_weight, image_ids):

    def row_grads(running, row_data):
        query_r, key_r, value_r, grads_r, ids_r = row_data
        token_ids = jnp.repeat(ids_r, BLK)
        grad_attn = inner(grads_r, out_weight).astype(jnp.bfloat16)
        attended, grad_query, grad_key, grad_value = all_heads(query_r, key_r, value_r, grad_attn, token_ids, token_ids, HEADS)
        running = running + outer(attended, grads_r)
        return (running, (grad_query.astype(jnp.bfloat16), grad_key.astype(jnp.bfloat16), grad_value.astype(jnp.bfloat16)))
    start_sum = jnp.zeros((D, D), jnp.float32)
    total, outputs = lax.scan(row_grads, start_sum, (queries, keys_in, value_rows, grad_out, image_ids))
    grad_weight = total * (1.0 / math.sqrt(TOKENS))
    return (outputs[0], outputs[1], outputs[2], grad_weight)
```

```python
import math

import jax
import jax.numpy as jnp
from jax import lax
from jax.experimental import pallas as pl
from jax.experimental.pallas import tpu as pltpu
from jax.sharding import PartitionSpec as P

HEADS = 16
BLK = 128
DH = 80
PAIR = 2 * DH
BIG = 12
GBLOCKS = 16
REST = GBLOCKS - BIG
CHUNK = 256
bf16 = jnp.bfloat16
f32 = jnp.float32


def nn(left, right):
    return lax.dot_general(left, right, (((1,), (0,)), ((), ())), preferred_element_type=f32)


def nt(left, right):
    return lax.dot_general(left, right, (((1,), (1,)), ((), ())), preferred_element_type=f32)


def pack_kernel(weight_ref, grads_ref, query_ref, key_ref, value_ref, out_ref):
    arrays = [
        query_ref[...].T,
        key_ref[...].T,
        value_ref[...].T,
        nt(weight_ref[...], grads_ref[...]).astype(bf16),
    ]
    for dest in range(out_ref.shape[0]):
        for block in range(2):
            for which, array in enumerate(arrays):
                out_ref[dest, block, which] = array[
                    dest * PAIR : (dest + 1) * PAIR, block * BLK : (block + 1) * BLK
                ]


def pack(weight, grads, query, key, value):
    rows, width = query.shape
    half = width // 2
    column = pl.BlockSpec((rows, half), lambda i: (0, i))
    return pl.pallas_call(
        pack_kernel,
        grid=(2,),
        in_specs=[
            pl.BlockSpec((half, width), lambda i: (i, 0)),
            pl.BlockSpec((rows, width), lambda i: (0, 0)),
            column,
            column,
            column,
        ],
        out_specs=pl.BlockSpec((4, 2, 4, PAIR, BLK), lambda i: (i, 0, 0, 0, 0)),
        out_shape=jax.ShapeDtypeStruct((8, 2, 4, PAIR, BLK), bf16),
        compiler_params=pltpu.CompilerParams(vmem_limit_bytes=48 * 2**20),
        cost_estimate=pl.CostEstimate(
            flops=2 * rows * width * width, bytes_accessed=9 * 2**20, transcendentals=0
        ),
        name="pack_heads",
    )(weight, grads, query, key, value)


def first_big(ids_ref):
    middle = ids_ref[0, GBLOCKS // 2]
    start = jnp.int32(0)
    for i in range(REST):
        start = start + (ids_ref[0, i] < middle).astype(jnp.int32)
    return start


def three_terms(row):
    high = row.astype(bf16).astype(f32)
    middle = (row - high).astype(bf16).astype(f32)
    low = row - high - middle
    zeros = jnp.zeros((BLK - DH - 3, row.shape[1]), f32)
    return jnp.concatenate([high, middle, low, zeros], axis=0).astype(bf16)


def attention_kernel(ids_ref, in_ref, att_ref, out_ref, rows_ref, kv_ref, acc_ref, mixed_ref):
    scale = 1.0 / math.sqrt(DH)
    log2e = 1.4426950408889634
    start = first_big(ids_ref)
    ones = (lax.broadcasted_iota(jnp.int32, (BLK - DH, BLK * GBLOCKS), 0) < 3).astype(bf16)
    zeros = jnp.zeros((BLK - DH, BLK * GBLOCKS), bf16)

    def place(slot):
        if slot < BIG:
            return start + slot
        other = slot - BIG
        return jnp.where(other < start, other, slot)

    for head in range(2):
        features = slice(head * DH, (head + 1) * DH)
        for which in range(4):
            rows_ref[head, which, DH:, :] = ones if which == 2 else zeros
        for slot in range(GBLOCKS):
            block = place(slot)
            for which in range(4):
                rows_ref[head, which, :DH, slot * BLK : (slot + 1) * BLK] = in_ref[
                    block, which, features, :
                ]
        kv_ref[head, 0] = rows_ref[head, 1].T
        kv_ref[head, 1] = rows_ref[head, 2].T

    def step(head, queries, keys, length, bias):
        span = pl.ds(keys, length)
        query_t = rows_ref[head, 0, :, queries]
        scores = nn(kv_ref[head, 0, span, :], query_t)
        if bias is not None:
            scores = scores + bias
        top = jnp.max(scores, axis=0, keepdims=True)
        weights = jnp.exp2((scores - top) * (scale * log2e))
        weights_low = weights.astype(bf16)
        mixed = nn(rows_ref[head, 2, : DH + 16, span], weights_low)
        inverse = 1.0 / mixed[DH : DH + 1]
        attended = (mixed[:DH] * inverse).astype(bf16)
        grads = (rows_ref[head, 3, :DH, queries].astype(f32) * inverse).astype(bf16)
        delta = -jnp.sum(grads.astype(f32) * attended.astype(f32), axis=0, keepdims=True)
        grads_more = jnp.concatenate(
            [grads, three_terms(delta)], axis=0
        )
        dscores = (weights * nn(kv_ref[head, 1, span, :], grads_more)).astype(bf16)
        mixed_ref[head * DH : (head + 1) * DH, queries] = attended
        grad_query = nn(rows_ref[head, 1, :DH, span], dscores) * scale
        acc_ref[head, 0, :, queries] = grad_query
        acc_ref[head, 1, :, span] += nt(query_t[:DH], dscores)
        acc_ref[head, 2, :, span] += nt(grads, weights_low)

    acc_ref[:, 1:] = jnp.zeros((2, 2, DH, BLK * GBLOCKS), f32)

    def big_step(i, carry):
        for head in range(2):
            step(head, pl.ds(pl.multiple_of(i * CHUNK, CHUNK), CHUNK), 0, BIG * BLK, None)
        return carry

    lax.fori_loop(0, BIG * BLK // CHUNK, big_step, 0)

    numbers = [ids_ref[0, place(BIG + i)] for i in range(REST)]

    def bias_of(first):
        columns = []
        for q in range(first, first + CHUNK // BLK):
            rows = [
                jnp.full((BLK, BLK), jnp.where(numbers[q] == numbers[k], 0.0, -1e30), f32)
                for k in range(REST)
            ]
            columns.append(jnp.concatenate(rows, axis=0))
        return jnp.concatenate(columns, axis=1)

    for part in range(REST * BLK // CHUNK):
        bias = bias_of(part * (CHUNK // BLK))
        for head in range(2):
            step(head, slice(BIG * BLK + part * CHUNK, BIG * BLK + (part + 1) * CHUNK), BIG * BLK, REST * BLK, bias)

    for head in range(2):
        features = slice(head * DH, (head + 1) * DH)
        for slot in range(GBLOCKS):
            block = place(slot)
            columns = slice(slot * BLK, (slot + 1) * BLK)
            out_ref[block, 0, features, :] = acc_ref[head, 0, :, columns].astype(bf16)
            out_ref[block, 1, features, :] = (acc_ref[head, 1, :, columns] * scale).astype(bf16)
            out_ref[block, 2, features, :] = acc_ref[head, 2, :, columns].astype(bf16)
    for slot in range(GBLOCKS):
        target = pl.ds(pl.multiple_of(place(slot) * BLK, BLK), BLK)
        att_ref[:, target] = mixed_ref[:, slot * BLK : (slot + 1) * BLK]


def attention(ids, packed):
    tokens = GBLOCKS * BLK
    return pl.pallas_call(
        attention_kernel,
        in_specs=[
            pl.BlockSpec(memory_space=pltpu.SMEM),
            pl.BlockSpec(memory_space=pltpu.VMEM),
        ],
        out_specs=[
            pl.BlockSpec(memory_space=pltpu.VMEM),
            pl.BlockSpec(memory_space=pltpu.VMEM),
        ],
        out_shape=[
            jax.ShapeDtypeStruct((PAIR, tokens), bf16),
            jax.ShapeDtypeStruct((GBLOCKS, 3, PAIR, BLK), bf16),
        ],
        scratch_shapes=[
            pltpu.VMEM((2, 4, BLK, tokens), bf16),
            pltpu.VMEM((2, 2, tokens, BLK), bf16),
            pltpu.VMEM((2, 3, DH, tokens), f32),
            pltpu.VMEM((PAIR, tokens), bf16),
        ],
        compiler_params=pltpu.CompilerParams(vmem_limit_bytes=56 * 2**20),
        cost_estimate=pl.CostEstimate(
            flops=2 * 6 * 2 * 160 * BLK * BLK * BLK, bytes_accessed=5 * 2**20, transcendentals=2 * 160 * BLK * BLK
        ),
        name="attention_grads",
    )(ids, packed)


def unpack_kernel(in_ref, *out_refs):
    for which, out_ref in enumerate(out_refs):
        for block in range(2):
            columns = jnp.concatenate([in_ref[src, block, which] for src in range(8)], axis=0)
            out_ref[block * BLK : (block + 1) * BLK, :] = columns.T


def unpack(received):
    count = received.shape[2]
    width = 8 * PAIR
    return pl.pallas_call(
        unpack_kernel,
        out_shape=[jax.ShapeDtypeStruct((2 * BLK, width), bf16)] * count,
        compiler_params=pltpu.CompilerParams(vmem_limit_bytes=48 * 2**20),
        cost_estimate=pl.CostEstimate(flops=0, bytes_accessed=4 * 2**20, transcendentals=0),
        name="unpack_heads",
    )(received)


CROWS = 112


def weight_kernel(att_ref, grads_ref, out_ref):
    product = nn(att_ref[...], grads_ref[...])
    columns = product.shape[1] // BLK
    for j in range(columns):
        out_ref[j * PAIR : (j + 1) * PAIR, :] = product[:, j * BLK : (j + 1) * BLK].astype(bf16)
    out_ref[columns * PAIR :, :] = jnp.zeros((out_ref.shape[0] - columns * PAIR, BLK), bf16)


def weight_terms(att, grads):
    return pl.pallas_call(
        weight_kernel,
        out_shape=jax.ShapeDtypeStruct((16 * CROWS, BLK), bf16),
        compiler_params=pltpu.CompilerParams(vmem_limit_bytes=48 * 2**20),
        cost_estimate=pl.CostEstimate(
            flops=2 * att.shape[0] * att.shape[1] * grads.shape[1], bytes_accessed=6 * 2**20, transcendentals=0
        ),
        name="weight_terms",
    )(att, grads)


def finish_kernel(core_ref, own_ref, other_ref, out_ref, rows_ref, *, scale):
    core = core_ref[0]
    for k in range(8):
        rows_ref[2 * k + core] = own_ref[0, k]
        rows_ref[2 * k + 1 - core] = other_ref[0, k]
    rows = rows_ref[...].reshape(16 * CROWS, BLK)
    for j in range(out_ref.shape[1] // BLK):
        block = rows[j * PAIR : (j + 1) * PAIR, :].astype(f32)
        out_ref[:, j * BLK : (j + 1) * BLK] = block * scale


def finish(core, own, other, scale):
    width = 8 * PAIR
    part = pl.BlockSpec((1, 8, CROWS, BLK), lambda i: (i, 0, 0, 0))
    return pl.pallas_call(
        lambda *refs: finish_kernel(*refs, scale=scale),
        grid=(8,),
        in_specs=[pl.BlockSpec(memory_space=pltpu.SMEM), part, part],
        out_specs=pl.BlockSpec((PAIR, width), lambda i: (i, 0)),
        out_shape=jax.ShapeDtypeStruct((width, width), f32),
        scratch_shapes=[pltpu.VMEM((16, CROWS, BLK), bf16)],
        cost_estimate=pl.CostEstimate(flops=0, bytes_accessed=10 * 2**20, transcendentals=0),
        name="finish_weight",
    )(core, own, other)


def per_device(queries, keys_in, value_rows, grad_out, out_weight, image_ids):
    grads_own = grad_out[0]
    packed = pack(out_weight, grads_own, queries[0], keys_in[0], value_rows[0])
    grads_all = lax.all_gather(grads_own, "grp", axis=0, tiled=True)
    received = lax.all_to_all(packed, "grp", 0, 0, tiled=True)
    att, out = attention(image_ids, received.reshape(GBLOCKS, 4, PAIR, BLK))
    back = lax.all_to_all(out.reshape(8, 2, 3, PAIR, BLK), "grp", 0, 0, tiled=True)
    grad_query, grad_key, grad_value = unpack(back)
    terms = weight_terms(att, grads_all).reshape(16, CROWS, BLK)
    parts = lax.all_to_all(terms, "dp", 0, 0, tiled=True)
    part = jnp.sum(parts.astype(f32), axis=0).astype(bf16)
    copies = jnp.broadcast_to(part[None], (64, CROWS, BLK))
    groups = [[i * 2 + core for i in range(64)] for core in range(2)]
    own = lax.all_to_all(copies, ("grp", "dp"), 0, 0, axis_index_groups=groups, tiled=True)
    other = lax.ppermute(own, "dp", [(i, i ^ 1) for i in range(16)])
    core = (lax.axis_index("dp") % 2).astype(jnp.int32).reshape(1)
    shape = (8, 8, CROWS, BLK)
    total = 2 * BLK * 8 * 16
    grad_weight = finish(core, own.reshape(shape), other.reshape(shape), 1.0 / math.sqrt(total))
    return (grad_query[None], grad_key[None], grad_value[None], grad_weight)


def solution(mesh):
    return jax.shard_map(
        per_device,
        mesh=mesh,
        in_specs=(
            P("dp", "grp", None),
            P("dp", "grp", None),
            P("dp", "grp", None),
            P("dp", "grp", None),
            P(),
            P("dp", None),
        ),
        out_specs=(P("dp", "grp", None), P("dp", "grp", None), P("dp", "grp", None), P()),
        check_vma=False,
    )
```

```python
import math

import jax
import jax.numpy as jnp
from jax import lax
from jax.experimental import pallas as pl
from jax.experimental.pallas import tpu as pltpu
from jax.sharding import PartitionSpec as P

HEADS = 16
BLK = 128
DH = 80
PAIR = 2 * DH
BIG = 12
GBLOCKS = 16
REST = GBLOCKS - BIG
BIG_CHUNK = 768
CHUNK = 512
SCALE = 1.0 / math.sqrt(DH)
LOG2E = 1.4426950408889634
WEIGHT_SCALE = 1.0 / math.sqrt(16 * GBLOCKS * BLK)
bf16 = jnp.bfloat16
f32 = jnp.float32


def nn(left, right):
    return lax.dot_general(left, right, (((1,), (0,)), ((), ())), preferred_element_type=f32)


def nt(left, right):
    return lax.dot_general(left, right, (((1,), (1,)), ((), ())), preferred_element_type=f32)


def whole(shape):
    return pl.BlockSpec(shape, lambda i: (0,) * len(shape))


def first_big(ids_ref):
    middle = ids_ref[0, GBLOCKS // 2]
    start = jnp.int32(0)
    for i in range(REST):
        start = start + (ids_ref[0, i] < middle).astype(jnp.int32)
    return start


def three_terms(row):
    high = row.astype(bf16).astype(f32)
    middle = (row - high).astype(bf16).astype(f32)
    low = row - high - middle
    zeros = jnp.zeros((BLK - DH - 3, row.shape[1]), f32)
    return jnp.concatenate([high, middle, low, zeros], axis=0).astype(bf16)


def place_of(start, slot):
    if slot < BIG:
        return start + slot
    other = slot - BIG
    return jnp.where(other < start, other, slot)


def slot_of(start, block):
    other = jnp.where(block < start, BIG + block, block)
    return jnp.where((block >= start) & (block < start + BIG), block - start, other)


def columns_of(slot):
    return slice(slot * BLK, (slot + 1) * BLK)


def pack_kernel(weight_ref, grads_ref, query_ref, key_ref, value_ref, *refs):
    out_ref, *half_refs = refs[-3:]
    arrays = [
        query_ref[...].T,
        key_ref[...].T,
        value_ref[...].T,
        nt(weight_ref[...], grads_ref[...]).astype(bf16),
    ]
    for dest in range(out_ref.shape[0]):
        for block in range(2):
            for which, array in enumerate(arrays):
                out_ref[dest, block, which] = array[
                    dest * DH : (dest + 1) * DH, columns_of(block)
                ]
    for i, half_ref in enumerate(half_refs):
        half_ref[...] = grads_ref[columns_of(i), :]


def pack(half, weight, grads, query, key, value, *after):
    rows, width = query.shape
    column = pl.BlockSpec((rows, width // 2), lambda i: (0, half))
    shapes = [
        jax.ShapeDtypeStruct((8, 2, 4, DH, BLK), bf16),
        jax.ShapeDtypeStruct((BLK, grads.shape[1]), bf16),
        jax.ShapeDtypeStruct((BLK, grads.shape[1]), bf16),
    ]
    return pl.pallas_call(
        pack_kernel,
        grid=(1,),
        in_specs=[
            pl.BlockSpec((width // 2, width), lambda i: (half, 0)),
            whole(grads.shape),
            column,
            column,
            column,
        ]
        + [pl.BlockSpec(memory_space=pl.ANY)] * len(after),
        out_specs=[whole(shape.shape) for shape in shapes],
        out_shape=shapes,
        compiler_params=pltpu.CompilerParams(vmem_limit_bytes=63 * 2**20),
        cost_estimate=pl.CostEstimate(
            flops=rows * width * width, bytes_accessed=5 * 2**20, transcendentals=0
        ),
        name="pack_heads",
    )(weight, grads, query, key, value, *after)


def attention_kernel(ids_ref, me_ref, in_ref, *refs):
    keep_ref, send_ref, out_ref, rows_ref, kv_ref, acc_ref, mixed_ref = refs[-7:]
    start = first_big(ids_ref)
    width = BLK * GBLOCKS
    ones = (lax.broadcasted_iota(jnp.int32, (BLK - DH, width), 0) < 3).astype(bf16)
    zeros = jnp.zeros((BLK - DH, width), bf16)
    for which in range(4):
        rows_ref[which, DH:, :] = ones if which == 2 else zeros
    for slot in range(GBLOCKS):
        block = place_of(start, slot)
        for which in range(4):
            rows_ref[which, :DH, columns_of(slot)] = in_ref[block, which]
    kv_ref[0] = rows_ref[1].T
    kv_ref[1] = rows_ref[2].T
    acc_ref[1:] = jnp.zeros((2, DH, width), f32)

    def chunk(queries, span, bias):
        query_t = rows_ref[0, :, queries]
        scores = nn(kv_ref[0, span, :], query_t)
        if bias is not None:
            scores = scores + bias
        top = jnp.max(scores, axis=0, keepdims=True)
        weights = jnp.exp2((scores - top) * (SCALE * LOG2E))
        weights_low = weights.astype(bf16)
        mixed = nn(rows_ref[2, : DH + 16, span], weights_low)
        inverse = 1.0 / mixed[DH : DH + 1]
        attended = (mixed[:DH] * inverse).astype(bf16)
        mixed_ref[:, queries] = attended
        grads = (rows_ref[3, :DH, queries].astype(f32) * inverse).astype(bf16)
        delta = -jnp.sum(grads.astype(f32) * attended.astype(f32), axis=0, keepdims=True)
        grads_more = jnp.concatenate([grads, three_terms(delta)], axis=0)
        dscores = (weights * nn(kv_ref[1, span, :], grads_more)).astype(bf16)
        acc_ref[0, :, queries] = nn(rows_ref[1, :DH, span], dscores)
        acc_ref[1, :, span] += nt(query_t[:DH], dscores)
        acc_ref[2, :, span] += nt(grads, weights_low)

    def big_chunk(i, carry):
        chunk(pl.ds(pl.multiple_of(i * BIG_CHUNK, BIG_CHUNK), BIG_CHUNK), slice(0, BIG * BLK), None)
        return carry

    lax.fori_loop(0, BIG * BLK // BIG_CHUNK, big_chunk, 0, unroll=2)

    numbers = [ids_ref[0, place_of(start, BIG + i)] for i in range(REST)]
    for part in range(REST * BLK // CHUNK):
        first = part * (CHUNK // BLK)
        columns = []
        for q in range(first, first + CHUNK // BLK):
            rows = [
                jnp.full((BLK, BLK), jnp.where(numbers[q] == numbers[k], 0.0, -1e30), f32)
                for k in range(REST)
            ]
            columns.append(jnp.concatenate(rows, axis=0))
        queries = slice(BIG * BLK + part * CHUNK, BIG * BLK + (part + 1) * CHUNK)
        chunk(queries, slice(BIG * BLK, GBLOCKS * BLK), jnp.concatenate(columns, axis=1))

    for slot in range(GBLOCKS):
        block = place_of(start, slot)
        own = lax.rem(lax.div(block, 2), 2) == lax.rem(me_ref[0], 2)
        column = lax.div(block, 4) * 2 + lax.rem(block, 2)
        target = pl.ds(pl.multiple_of(column * BLK, BLK), BLK)

        @pl.when(own)
        def _():
            keep_ref[:, target] = mixed_ref[:, columns_of(slot)]

        @pl.when(jnp.logical_not(own))
        def _():
            send_ref[:, target] = mixed_ref[:, columns_of(slot)]

    for slot in range(GBLOCKS):
        block = place_of(start, slot)
        for which in range(3):
            part = acc_ref[which, :, columns_of(slot)]
            if which < 2:
                part = part * SCALE
            out_ref[block, which] = part.astype(bf16)


def attention(head, ids, me, packed, *before):
    tokens = GBLOCKS * BLK
    shapes = [jax.ShapeDtypeStruct((PAIR, tokens // 2), bf16)] * 2
    shapes += [jax.ShapeDtypeStruct((GBLOCKS, 3, PAIR, BLK), bf16)]
    smem = pl.BlockSpec(memory_space=pltpu.SMEM)
    blocks = [pl.BlockSpec((DH, tokens // 2), lambda i: (head, 0))] * 2
    blocks += [pl.BlockSpec((GBLOCKS, 3, DH, BLK), lambda i: (0, 0, head, 0))]
    return pl.pallas_call(
        attention_kernel,
        grid=(1,),
        in_specs=[smem, smem, whole(packed.shape)]
        + [pl.BlockSpec(memory_space=pl.ANY)] * len(before),
        out_specs=blocks,
        out_shape=shapes,
        input_output_aliases={3 + i: i for i in range(len(before))},
        scratch_shapes=[
            pltpu.VMEM((4, BLK, tokens), bf16),
            pltpu.VMEM((2, tokens, BLK), bf16),
            pltpu.VMEM((3, DH, tokens), f32),
            pltpu.VMEM((DH, tokens), bf16),
        ],
        compiler_params=pltpu.CompilerParams(vmem_limit_bytes=63 * 2**20),
        cost_estimate=pl.CostEstimate(
            flops=2 * 6 * 3 * 160 * BLK * BLK * BLK,
            bytes_accessed=4 * 2**20,
            transcendentals=160 * BLK * BLK,
        ),
        name="attention_grads",
    )(ids, me, packed, *before)


def unpack_kernel(in_ref, *out_refs):
    for which, out_ref in enumerate(out_refs):
        for half in range(2):
            rows = [
                in_ref[source, half, which, head * DH : (head + 1) * DH, :]
                for head in range(2)
                for source in range(8)
            ]
            out_ref[half * BLK : (half + 1) * BLK, :] = jnp.concatenate(rows, axis=0).T


def unpack(received):
    count = received.shape[2]
    width = 8 * PAIR
    return pl.pallas_call(
        unpack_kernel,
        out_shape=[jax.ShapeDtypeStruct((2 * BLK, width), bf16)] * count,
        compiler_params=pltpu.CompilerParams(vmem_limit_bytes=63 * 2**20),
        cost_estimate=pl.CostEstimate(flops=0, bytes_accessed=4 * 2**20, transcendentals=0),
        name="unpack_heads",
    )(received)


CROWS = 112


def weight_kernel(me_ref, column_ref, keep_ref, other_ref, *refs):
    grads_refs, out_refs, both_ref, ring_ref, rows_ref = refs[:-5], refs[-5:-3], *refs[-3:-1], refs[-1]
    core = lax.rem(column_ref[0], 2)
    low = lax.rem(lax.div(column_ref[0], 2), 2)
    z = lax.div(column_ref[0], 4)
    both_ref[:PAIR] = keep_ref[...]
    both_ref[PAIR:] = other_ref[...]
    gx = lax.div(me_ref[0], 2)
    offset = gx * (2 * BLK)
    first = 0
    for grads_ref in grads_refs:
        rows = grads_ref.shape[0]
        columns = pl.ds(pl.multiple_of(lax.rem(offset, both_ref.shape[1]), BLK), rows)
        ring_ref[:, first : first + rows] = both_ref[:, columns]
        offset = offset + rows
        first = first + rows
    left = ring_ref[...]
    width = grads_refs[0].shape[1]
    blocks = []
    for j in range(0, width, 2 * BLK):
        right = jnp.concatenate([ref[:, j : j + 2 * BLK] for ref in grads_refs], axis=0)
        blocks.append(nn(left, right).astype(bf16))
    product = jnp.concatenate(blocks, axis=1)
    per_core = product.shape[1] // BLK // 2
    for which in range(2):
        for half in range(2):
            for j in range(per_core):
                rows_ref[j * PAIR : (j + 1) * PAIR, :] = product[
                    which * PAIR : (which + 1) * PAIR, columns_of(half * per_core + j)
                ]
            rows_ref[per_core * PAIR :, :] = jnp.zeros((8 * CROWS - per_core * PAIR, BLK), bf16)

            def store(out_ref):
                for j in range(8):
                    along_z = lax.bitwise_xor(z, j // 2)
                    along_y = which * 2 + lax.bitwise_xor(low, j % 2)
                    out_ref[along_z, along_y] = rows_ref[j * CROWS : (j + 1) * CROWS, :]

            pl.when(core == half)(lambda: store(out_refs[0]))
            pl.when(core != half)(lambda: store(out_refs[1]))


def weight_terms(me, column, keep, other, grads):
    vmem = pl.BlockSpec(memory_space=pltpu.VMEM)
    return pl.pallas_call(
        weight_kernel,
        in_specs=[pl.BlockSpec(memory_space=pltpu.SMEM)] * 2 + [vmem] * (2 + len(grads)),
        out_specs=[vmem] * 2,
        out_shape=[jax.ShapeDtypeStruct((4, 4, CROWS, BLK), bf16)] * 2,
        scratch_shapes=[
            pltpu.VMEM((2 * PAIR, keep.shape[1]), bf16),
            pltpu.VMEM((2 * PAIR, keep.shape[1]), bf16),
            pltpu.VMEM((8 * CROWS, BLK), bf16),
        ],
        compiler_params=pltpu.CompilerParams(vmem_limit_bytes=63 * 2**20),
        cost_estimate=pl.CostEstimate(
            flops=2 * 2 * PAIR * 4 * grads[0].size, bytes_accessed=6 * 2**20, transcendentals=0
        ),
        name="weight_terms",
    )(me, column, keep, other, *grads)


def add_kernel(*refs):
    count = len(refs) - 4
    for i in range(4):
        total = refs[0][i].astype(f32)
        for ref in refs[1:count]:
            total = total + ref[i].astype(f32)
        refs[count + i][...] = total.astype(bf16)


def add_up(*arrays):
    shape = arrays[0].shape[1:]
    return pl.pallas_call(
        add_kernel,
        out_shape=[jax.ShapeDtypeStruct(shape, bf16)] * 4,
        compiler_params=pltpu.CompilerParams(vmem_limit_bytes=63 * 2**20),
        cost_estimate=pl.CostEstimate(
            flops=len(arrays) * arrays[0].size, bytes_accessed=2**20, transcendentals=0
        ),
        name="add_up",
    )(*arrays)


def nothing_kernel(*refs):
    pass


def once(array, *after):
    anywhere = pl.BlockSpec(memory_space=pl.ANY)
    return pl.pallas_call(
        nothing_kernel,
        in_specs=[anywhere] * (1 + len(after)),
        out_specs=anywhere,
        out_shape=jax.ShapeDtypeStruct(array.shape, array.dtype),
        input_output_aliases={0: 0},
        compiler_params=pltpu.CompilerParams(vmem_limit_bytes=63 * 2**20),
        name="once",
    )(array, *after)


def add_kernel(*refs):
    count = len(refs) - 4
    for i in range(4):
        total = refs[0][i].astype(f32)
        for ref in refs[1:count]:
            total = total + ref[i].astype(f32)
        refs[count + i][...] = total.astype(bf16)


def add_up(*arrays):
    shape = arrays[0].shape[1:]
    return pl.pallas_call(
        add_kernel,
        out_shape=[jax.ShapeDtypeStruct(shape, bf16)] * 4,
        compiler_params=pltpu.CompilerParams(vmem_limit_bytes=63 * 2**20),
        cost_estimate=pl.CostEstimate(
            flops=len(arrays) * arrays[0].size, bytes_accessed=2**20, transcendentals=0
        ),
        name="add_up",
    )(*arrays)


def nothing_kernel(*refs):
    pass


def once(array, *after):
    anywhere = pl.BlockSpec(memory_space=pl.ANY)
    return pl.pallas_call(
        nothing_kernel,
        in_specs=[anywhere] * (1 + len(after)),
        out_specs=anywhere,
        out_shape=jax.ShapeDtypeStruct(array.shape, array.dtype),
        input_output_aliases={0: 0},
        compiler_params=pltpu.CompilerParams(vmem_limit_bytes=63 * 2**20),
        name="once",
    )(array, *after)


def finish_kernel(core_ref, in_ref, *refs):
    out_ref = refs[-1]
    for pair in range(in_ref.shape[0]):
        for j in range(out_ref.shape[3] // BLK):
            block = in_ref[pair, j * PAIR : (j + 1) * PAIR, :].astype(f32) * WEIGHT_SCALE
            for head in range(2):
                out_ref[head, pair, :, columns_of(j)] = block[head * DH : (head + 1) * DH]


def finish(core, rows, *before):
    width = 8 * PAIR
    return pl.pallas_call(
        finish_kernel,
        grid_spec=pltpu.PrefetchScalarGridSpec(
            num_scalar_prefetch=1,
            grid=(2,),
            in_specs=[pl.BlockSpec((4, 8 * CROWS, BLK), lambda i, core: (i, 0, 0))]
            + [pl.BlockSpec(memory_space=pl.ANY)] * len(before),
            out_specs=pl.BlockSpec((2, 4, DH, width // 2), lambda i, core: (0, i, 0, core[0])),
        ),
        out_shape=jax.ShapeDtypeStruct((2, 8, DH, width), f32),
        input_output_aliases={2: 0} if before else {},
        compiler_params=pltpu.CompilerParams(vmem_limit_bytes=63 * 2**20),
        cost_estimate=pl.CostEstimate(flops=0, bytes_accessed=5 * 2**20, transcendentals=0),
        name="finish_weight",
    )(core, rows, *before)


def scalar(value):
    return value.astype(jnp.int32).reshape(1)


def per_device(queries, keys_in, value_rows, grad_out, out_weight, image_ids):
    grads_own = grad_out[0]
    both = ("grp", "dp")
    me = scalar(lax.axis_index("grp"))
    core = lax.axis_index("dp") % 2
    operands = (out_weight, grads_own, queries[0], keys_in[0], value_rows[0])
    packed_first, _, _ = pack(0, *operands)
    packed_second, *grads_late = pack(1, *operands, packed_first)
    shape = (GBLOCKS, 4, DH, BLK)
    first = lax.all_to_all(packed_first, "grp", 0, 0, tiled=True).reshape(shape)
    packed_second = once(packed_second, first)
    second = lax.all_to_all(packed_second, "grp", 0, 0, tiled=True).reshape(shape)
    results = attention(0, image_ids, me, first)
    up = [(i, (i + 2) % 8) for i in range(8)]
    down = [(i, (i + 6) % 8) for i in range(8)]
    grads_late = [once(half, first) for half in grads_late]
    grads_left = [lax.ppermute(half, "grp", up) for half in grads_late]
    grads_right = [lax.ppermute(half, "grp", down) for half in grads_late]
    keep, send, out = attention(1, image_ids, me, second, *results)
    grads_right[0] = once(grads_right[0], send)
    grads_left[1] = once(grads_left[1], send)
    grads_far = [lax.ppermute(grads_right[0], "grp", down), lax.ppermute(grads_left[1], "grp", up)]
    send = once(send, *grads_left, *grads_right)
    other = lax.ppermute(send, "grp", [(i, i ^ 1) for i in range(8)])
    out = once(out, other, *grads_far)
    back = lax.all_to_all(out.reshape(8, 2, 3, PAIR, BLK), "grp", 0, 0, tiled=True)
    grads_line = (grads_own, *grads_right, *grads_far, *grads_left)
    column = scalar(lax.axis_index("dp"))
    kept, sent = weight_terms(me, column, keep, other, grads_line)
    cores = [(i, i ^ 1) for i in range(16)]
    sent = lax.ppermute(sent, "dp", cores)
    parts = [(kept[k].astype(f32) + sent[k].astype(f32)).astype(bf16) for k in range(4)]
    parts = [parts[0]] + [
        lax.ppermute(parts[k], "dp", [(i, i ^ (4 * k)) for i in range(16)]) for k in range(1, 4)
    ]
    parts = [sum(item[k].astype(f32) for item in parts).astype(bf16) for k in range(4)]
    parts = [parts[0]] + [
        lax.ppermute(parts[k], both, [(i, i ^ (16 * (k // 2) + 2 * (k % 2))) for i in range(128)])
        for k in range(1, 4)
    ]
    part = sum(item.astype(f32) for item in parts).astype(bf16)
    copies = jnp.broadcast_to(part[None], (64,) + part.shape)
    same_core = [[i * 2 + c for i in range(64)] for c in range(2)]
    own = lax.all_to_all(copies, both, 0, 0, axis_index_groups=same_core, tiled=True)
    grad_query, grad_key, grad_value = unpack(back)
    own = once(own, grad_query).reshape(8, 8 * CROWS, BLK)
    swapped = lax.ppermute(own, "dp", cores)
    grad_weight = finish(scalar(1 - core), swapped, finish(scalar(core), own))
    grad_weight = grad_weight.reshape(out_weight.shape)
    return (grad_query[None], grad_key[None], grad_value[None], grad_weight)


def solution(mesh):
    return jax.shard_map(
        per_device,
        mesh=mesh,
        in_specs=(
            P("dp", "grp", None),
            P("dp", "grp", None),
            P("dp", "grp", None),
            P("dp", "grp", None),
            P(),
            P("dp", None),
        ),
        out_specs=(P("dp", "grp", None), P("dp", "grp", None), P("dp", "grp", None), P()),
        check_vma=False,
    )
```

```python
import math

import jax
import jax.numpy as jnp
from jax import lax
from jax.experimental import pallas as pl
from jax.experimental.pallas import tpu as pltpu
from jax.sharding import PartitionSpec as P

HEADS = 16
BLK = 128
DH = 80
PAIR = 2 * DH
BIG = 12
GBLOCKS = 16
REST = GBLOCKS - BIG
BIG_CHUNK = 768
CHUNK = 512
SCALE = 1.0 / math.sqrt(DH)
LOG2E = 1.4426950408889634
WEIGHT_SCALE = 1.0 / math.sqrt(16 * GBLOCKS * BLK)
bf16 = jnp.bfloat16
f32 = jnp.float32


def nn(left, right):
    return lax.dot_general(left, right, (((1,), (0,)), ((), ())), preferred_element_type=f32)


def nt(left, right):
    return lax.dot_general(left, right, (((1,), (1,)), ((), ())), preferred_element_type=f32)


def whole(shape):
    return pl.BlockSpec(shape, lambda i: (0,) * len(shape))


def first_big(ids_ref):
    middle = ids_ref[0, GBLOCKS // 2]
    start = jnp.int32(0)
    for i in range(REST):
        start = start + (ids_ref[0, i] < middle).astype(jnp.int32)
    return start


def three_terms(row):
    high = row.astype(bf16).astype(f32)
    middle = (row - high).astype(bf16).astype(f32)
    low = row - high - middle
    zeros = jnp.zeros((BLK - DH - 3, row.shape[1]), f32)
    return jnp.concatenate([high, middle, low, zeros], axis=0).astype(bf16)


def place_of(start, slot):
    if slot < BIG:
        return start + slot
    other = slot - BIG
    return jnp.where(other < start, other, slot)


def slot_of(start, block):
    other = jnp.where(block < start, BIG + block, block)
    return jnp.where((block >= start) & (block < start + BIG), block - start, other)


def columns_of(slot):
    return slice(slot * BLK, (slot + 1) * BLK)


def pack_kernel(weight_ref, grads_ref, query_ref, key_ref, value_ref, *refs):
    out_ref, *half_refs = refs[-3:]
    arrays = [
        query_ref[...].T,
        key_ref[...].T,
        value_ref[...].T,
        nt(weight_ref[...], grads_ref[...]).astype(bf16),
    ]
    for dest in range(out_ref.shape[0]):
        for block in range(2):
            for which, array in enumerate(arrays):
                out_ref[dest, block, which] = array[
                    dest * DH : (dest + 1) * DH, columns_of(block)
                ]
    for i, half_ref in enumerate(half_refs):
        half_ref[...] = grads_ref[columns_of(i), :]


def pack(half, weight, grads, query, key, value, *after):
    rows, width = query.shape
    column = pl.BlockSpec((rows, width // 2), lambda i: (0, half))
    shapes = [
        jax.ShapeDtypeStruct((8, 2, 4, DH, BLK), bf16),
        jax.ShapeDtypeStruct((BLK, grads.shape[1]), bf16),
        jax.ShapeDtypeStruct((BLK, grads.shape[1]), bf16),
    ]
    return pl.pallas_call(
        pack_kernel,
        grid=(1,),
        in_specs=[
            pl.BlockSpec((width // 2, width), lambda i: (half, 0)),
            whole(grads.shape),
            column,
            column,
            column,
        ]
        + [pl.BlockSpec(memory_space=pltpu.HBM)] * len(after),
        out_specs=[whole(shape.shape) for shape in shapes],
        out_shape=shapes,
        compiler_params=pltpu.CompilerParams(vmem_limit_bytes=65408 * 2**10),
        cost_estimate=pl.CostEstimate(
            flops=rows * width * width, bytes_accessed=5 * 2**20, transcendentals=0
        ),
        name="pack_heads",
    )(weight, grads, query, key, value, *after)


def attention_kernel(ids_ref, me_ref, in_ref, *refs):
    keep_ref, send_ref, out_ref, rows_ref, kv_ref, acc_ref, mixed_ref = refs[-7:]
    start = first_big(ids_ref)
    width = BLK * GBLOCKS
    ones = (lax.broadcasted_iota(jnp.int32, (BLK - DH, width), 0) < 3).astype(bf16)
    zeros = jnp.zeros((BLK - DH, width), bf16)
    for which in range(4):
        rows_ref[which, DH:, :] = ones if which == 2 else zeros
    for slot in range(GBLOCKS):
        block = place_of(start, slot)
        for which in range(4):
            rows_ref[which, :DH, columns_of(slot)] = in_ref[block, which]
    kv_ref[0] = rows_ref[1].T
    kv_ref[1] = rows_ref[2].T
    acc_ref[1:] = jnp.zeros((2, DH, width), f32)

    def chunk(queries, span, bias):
        query_t = rows_ref[0, :, queries]
        scores = nn(kv_ref[0, span, :], query_t)
        if bias is not None:
            scores = scores + bias
        top = jnp.max(scores, axis=0, keepdims=True)
        weights = jnp.exp2((scores - top) * (SCALE * LOG2E))
        weights_low = weights.astype(bf16)
        mixed = nn(rows_ref[2, : DH + 16, span], weights_low)
        inverse = 1.0 / mixed[DH : DH + 1]
        attended = (mixed[:DH] * inverse).astype(bf16)
        mixed_ref[:, queries] = attended
        grads = (rows_ref[3, :DH, queries].astype(f32) * inverse).astype(bf16)
        delta = -jnp.sum(grads.astype(f32) * attended.astype(f32), axis=0, keepdims=True)
        grads_more = jnp.concatenate([grads, three_terms(delta)], axis=0)
        dscores = (weights * nn(kv_ref[1, span, :], grads_more)).astype(bf16)
        acc_ref[0, :, queries] = nn(rows_ref[1, :DH, span], dscores)
        acc_ref[1, :, span] += nt(query_t[:DH], dscores)
        acc_ref[2, :, span] += nt(grads, weights_low)

    def big_chunk(i, carry):
        chunk(pl.ds(pl.multiple_of(i * BIG_CHUNK, BIG_CHUNK), BIG_CHUNK), slice(0, BIG * BLK), None)
        return carry

    lax.fori_loop(0, BIG * BLK // BIG_CHUNK, big_chunk, 0, unroll=2)

    numbers = [ids_ref[0, place_of(start, BIG + i)] for i in range(REST)]
    for part in range(REST * BLK // CHUNK):
        first = part * (CHUNK // BLK)
        columns = []
        for q in range(first, first + CHUNK // BLK):
            rows = [
                jnp.full((BLK, BLK), jnp.where(numbers[q] == numbers[k], 0.0, -1e30), f32)
                for k in range(REST)
            ]
            columns.append(jnp.concatenate(rows, axis=0))
        queries = slice(BIG * BLK + part * CHUNK, BIG * BLK + (part + 1) * CHUNK)
        chunk(queries, slice(BIG * BLK, GBLOCKS * BLK), jnp.concatenate(columns, axis=1))

    for slot in range(GBLOCKS):
        block = place_of(start, slot)
        own = lax.rem(lax.div(block, 2), 2) == lax.rem(me_ref[0], 2)
        column = lax.div(block, 4) * 2 + lax.rem(block, 2)
        target = pl.ds(pl.multiple_of(column * BLK, BLK), BLK)

        @pl.when(own)
        def _():
            keep_ref[:, target] = mixed_ref[:, columns_of(slot)]

        @pl.when(jnp.logical_not(own))
        def _():
            send_ref[:, target] = mixed_ref[:, columns_of(slot)]

    for slot in range(GBLOCKS):
        block = place_of(start, slot)
        for which in range(3):
            part = acc_ref[which, :, columns_of(slot)]
            if which < 2:
                part = part * SCALE
            out_ref[block, which] = part.astype(bf16)


def attention(head, ids, me, packed, *before):
    tokens = GBLOCKS * BLK
    shapes = [jax.ShapeDtypeStruct((DH, tokens // 2), bf16)] * 2
    shapes += [jax.ShapeDtypeStruct((GBLOCKS, 3, PAIR, BLK), bf16)]
    smem = pl.BlockSpec(memory_space=pltpu.SMEM)
    blocks = [whole(shapes[0].shape)] * 2
    blocks += [pl.BlockSpec((GBLOCKS, 3, DH, BLK), lambda i: (0, 0, head, 0))]
    return pl.pallas_call(
        attention_kernel,
        grid=(1,),
        in_specs=[smem, smem, whole(packed.shape)]
        + [pl.BlockSpec(memory_space=pltpu.HBM)] * len(before),
        out_specs=blocks,
        out_shape=shapes,
        input_output_aliases={3: 2} if before else {},
        scratch_shapes=[
            pltpu.VMEM((4, BLK, tokens), bf16),
            pltpu.VMEM((2, tokens, BLK), bf16),
            pltpu.VMEM((3, DH, tokens), f32),
            pltpu.VMEM((DH, tokens), bf16),
        ],
        compiler_params=pltpu.CompilerParams(vmem_limit_bytes=65408 * 2**10),
        cost_estimate=pl.CostEstimate(
            flops=2 * 6 * 3 * 160 * BLK * BLK * BLK,
            bytes_accessed=4 * 2**20,
            transcendentals=160 * BLK * BLK,
        ),
        name="attention_grads",
    )(ids, me, packed, *before)


def unpack_kernel(in_ref, *out_refs):
    for which, out_ref in enumerate(out_refs):
        for half in range(2):
            rows = [
                in_ref[source, half, which, head * DH : (head + 1) * DH, :]
                for head in range(2)
                for source in range(8)
            ]
            out_ref[half * BLK : (half + 1) * BLK, :] = jnp.concatenate(rows, axis=0).T


def unpack(received):
    count = received.shape[2]
    width = 8 * PAIR
    return pl.pallas_call(
        unpack_kernel,
        out_shape=[jax.ShapeDtypeStruct((2 * BLK, width), bf16)] * count,
        compiler_params=pltpu.CompilerParams(vmem_limit_bytes=24 * 2**20),
        cost_estimate=pl.CostEstimate(flops=0, bytes_accessed=4 * 2**20, transcendentals=0),
        name="unpack_heads",
    )(received)


CROWS = 112


def weight_kernel(me_ref, column_ref, *refs):
    grads_refs, out_refs, both_ref, ring_ref, rows_ref = refs[4:-5], refs[-5:-3], *refs[-3:-1], refs[-1]
    core = lax.rem(column_ref[0], 2)
    low = lax.rem(lax.div(column_ref[0], 2), 2)
    z = lax.div(column_ref[0], 4)
    for i in range(4):
        both_ref[i * DH : (i + 1) * DH] = refs[i][...]
    gx = lax.div(me_ref[0], 2)
    offset = gx * (2 * BLK)
    first = 0
    for grads_ref in grads_refs:
        rows = grads_ref.shape[0]
        columns = pl.ds(pl.multiple_of(lax.rem(offset, both_ref.shape[1]), BLK), rows)
        ring_ref[:, first : first + rows] = both_ref[:, columns]
        offset = offset + rows
        first = first + rows
    left = ring_ref[...]
    width = grads_refs[0].shape[1]
    blocks = []
    for j in range(0, width, 2 * BLK):
        right = jnp.concatenate([ref[:, j : j + 2 * BLK] for ref in grads_refs], axis=0)
        blocks.append(nn(left, right).astype(bf16))
    product = jnp.concatenate(blocks, axis=1)
    per_core = product.shape[1] // BLK // 2
    for which in range(2):
        for half in range(2):
            for j in range(per_core):
                rows_ref[j * PAIR : (j + 1) * PAIR, :] = product[
                    which * PAIR : (which + 1) * PAIR, columns_of(half * per_core + j)
                ]
            rows_ref[per_core * PAIR :, :] = jnp.zeros((8 * CROWS - per_core * PAIR, BLK), bf16)

            def store(out_ref):
                for j in range(8):
                    along_z = lax.bitwise_xor(z, j // 2)
                    along_y = which * 2 + lax.bitwise_xor(low, j % 2)
                    out_ref[along_z, along_y] = rows_ref[j * CROWS : (j + 1) * CROWS, :]

            pl.when(core == half)(lambda: store(out_refs[0]))
            pl.when(core != half)(lambda: store(out_refs[1]))


def weight_terms(me, column, atts, grads):
    vmem = pl.BlockSpec(memory_space=pltpu.VMEM)
    return pl.pallas_call(
        weight_kernel,
        in_specs=[pl.BlockSpec(memory_space=pltpu.SMEM)] * 2 + [vmem] * (4 + len(grads)),
        out_specs=[vmem] * 2,
        out_shape=[jax.ShapeDtypeStruct((4, 4, CROWS, BLK), bf16)] * 2,
        scratch_shapes=[
            pltpu.VMEM((2 * PAIR, atts[0].shape[1]), bf16),
            pltpu.VMEM((2 * PAIR, atts[0].shape[1]), bf16),
            pltpu.VMEM((8 * CROWS, BLK), bf16),
        ],
        compiler_params=pltpu.CompilerParams(vmem_limit_bytes=65408 * 2**10),
        cost_estimate=pl.CostEstimate(
            flops=2 * 2 * PAIR * 4 * grads[0].size, bytes_accessed=6 * 2**20, transcendentals=0
        ),
        name="weight_terms",
    )(me, column, *atts, *grads)


def add_kernel(*refs):
    count = len(refs) - 4
    for i in range(4):
        total = refs[0][i].astype(f32)
        for ref in refs[1:count]:
            total = total + ref[i].astype(f32)
        refs[count + i][...] = total.astype(bf16)


def add_up(*arrays):
    shape = arrays[0].shape[1:]
    return pl.pallas_call(
        add_kernel,
        out_shape=[jax.ShapeDtypeStruct(shape, bf16)] * 4,
        compiler_params=pltpu.CompilerParams(vmem_limit_bytes=65408 * 2**10),
        cost_estimate=pl.CostEstimate(
            flops=len(arrays) * arrays[0].size, bytes_accessed=2**20, transcendentals=0
        ),
        name="add_up",
    )(*arrays)


def nothing_kernel(*refs):
    pass


def once(array, *after):
    anywhere = pl.BlockSpec(memory_space=pltpu.HBM)
    return pl.pallas_call(
        nothing_kernel,
        in_specs=[anywhere] * (1 + len(after)),
        out_specs=anywhere,
        out_shape=jax.ShapeDtypeStruct(array.shape, array.dtype),
        input_output_aliases={0: 0},
        compiler_params=pltpu.CompilerParams(vmem_limit_bytes=65408 * 2**10),
        cost_estimate=pl.CostEstimate(flops=0, bytes_accessed=0, transcendentals=0),
        name="once",
    )(array, *after)


def add_kernel(*refs):
    count = len(refs) - 4
    for i in range(4):
        total = refs[0][i].astype(f32)
        for ref in refs[1:count]:
            total = total + ref[i].astype(f32)
        refs[count + i][...] = total.astype(bf16)


def add_up(*arrays):
    shape = arrays[0].shape[1:]
    return pl.pallas_call(
        add_kernel,
        out_shape=[jax.ShapeDtypeStruct(shape, bf16)] * 4,
        compiler_params=pltpu.CompilerParams(vmem_limit_bytes=65408 * 2**10),
        cost_estimate=pl.CostEstimate(
            flops=len(arrays) * arrays[0].size, bytes_accessed=2**20, transcendentals=0
        ),
        name="add_up",
    )(*arrays)


def nothing_kernel(*refs):
    pass


def once(array, *after):
    anywhere = pl.BlockSpec(memory_space=pltpu.HBM)
    return pl.pallas_call(
        nothing_kernel,
        in_specs=[anywhere] * (1 + len(after)),
        out_specs=anywhere,
        out_shape=jax.ShapeDtypeStruct(array.shape, array.dtype),
        input_output_aliases={0: 0},
        compiler_params=pltpu.CompilerParams(vmem_limit_bytes=65408 * 2**10),
        cost_estimate=pl.CostEstimate(flops=0, bytes_accessed=0, transcendentals=0),
        name="once",
    )(array, *after)


def one_kernel(*refs):
    refs[-1][0, 0] = 1.0


def one_after(*after):
    return pl.pallas_call(
        one_kernel,
        in_specs=[pl.BlockSpec(memory_space=pltpu.HBM)] * len(after),
        out_specs=pl.BlockSpec(memory_space=pltpu.SMEM),
        out_shape=jax.ShapeDtypeStruct((1, 1), f32),
        cost_estimate=pl.CostEstimate(flops=0, bytes_accessed=0, transcendentals=0),
        name="one_after",
    )(*after)


def finish_kernel(core_ref, in_ref, *refs):
    out_ref = refs[-1]
    for pair in range(in_ref.shape[0]):
        for j in range(out_ref.shape[3] // BLK):
            block = in_ref[pair, j * PAIR : (j + 1) * PAIR, :].astype(f32) * WEIGHT_SCALE
            for head in range(2):
                out_ref[head, pair, :, columns_of(j)] = block[head * DH : (head + 1) * DH]


def finish(core, rows, *before):
    width = 8 * PAIR
    return pl.pallas_call(
        finish_kernel,
        grid_spec=pltpu.PrefetchScalarGridSpec(
            num_scalar_prefetch=1,
            grid=(2,),
            in_specs=[pl.BlockSpec((4, 8 * CROWS, BLK), lambda i, core: (i, 0, 0))]
            + [pl.BlockSpec(memory_space=pltpu.HBM)] * len(before),
            out_specs=pl.BlockSpec((2, 4, DH, width // 2), lambda i, core: (0, i, 0, core[0])),
        ),
        out_shape=jax.ShapeDtypeStruct((2, 8, DH, width), f32),
        input_output_aliases={2: 0} if before else {},
        compiler_params=pltpu.CompilerParams(vmem_limit_bytes=16 * 2**20),
        cost_estimate=pl.CostEstimate(flops=0, bytes_accessed=5 * 2**20, transcendentals=0),
        name="finish_weight",
    )(core, rows, *before)


def scalar(value):
    return value.astype(jnp.int32).reshape(1)


def per_device(queries, keys_in, value_rows, grad_out, out_weight, image_ids):
    grads_own = grad_out[0]
    both = ("grp", "dp")
    me = scalar(lax.axis_index("grp"))
    core = lax.axis_index("dp") % 2
    operands = (out_weight, grads_own, queries[0], keys_in[0], value_rows[0])
    packed_first, _, _ = pack(0, *operands)
    packed_second, *grads_late = pack(1, *operands, packed_first)
    shape = (GBLOCKS, 4, DH, BLK)
    first = lax.all_to_all(packed_first, "grp", 0, 0, tiled=True).reshape(shape)
    packed_second = once(packed_second, first)
    second = lax.all_to_all(packed_second, "grp", 0, 0, tiled=True).reshape(shape)
    keep_first, send_first, out = attention(0, image_ids, me, first)
    up = [(i, (i + 2) % 8) for i in range(8)]
    down = [(i, (i + 6) % 8) for i in range(8)]
    grads_late = [once(half, send_first) for half in grads_late]
    grads_left = [lax.ppermute(half, "grp", up) for half in grads_late]
    grads_right = [lax.ppermute(half, "grp", down) for half in grads_late]
    keep, send, out = attention(1, image_ids, me, second, out)
    side = [(i, i ^ 1) for i in range(8)]
    other_first = lax.ppermute(send_first, "grp", side)
    grads_right[0] = once(grads_right[0], send)
    grads_left[1] = once(grads_left[1], send)
    grads_far = [lax.ppermute(grads_right[0], "grp", down), lax.ppermute(grads_left[1], "grp", up)]
    send = once(send, *grads_left, *grads_right)
    send = once(send, other_first)
    other = lax.ppermute(send, "grp", side)
    out = once(out, other, *grads_far)
    back = lax.all_to_all(out.reshape(8, 2, 3, PAIR, BLK), "grp", 0, 0, tiled=True)
    grads_line = (grads_own, *grads_right, *grads_far, *grads_left)
    column = scalar(lax.axis_index("dp"))
    kept, sent = weight_terms(me, column, (keep_first, keep, other_first, other), grads_line)
    cores = [(i, i ^ 1) for i in range(16)]
    sent = lax.ppermute(sent, "dp", cores)
    parts = [(kept[k].astype(f32) + sent[k].astype(f32)).astype(bf16) for k in range(4)]
    parts = [parts[0]] + [
        lax.ppermute(parts[k], "dp", [(i, i ^ (4 * k)) for i in range(16)]) for k in range(1, 4)
    ]
    parts = [sum(item[k].astype(f32) for item in parts).astype(bf16) for k in range(4)]
    parts = [parts[0]] + [
        lax.ppermute(parts[k], both, [(i, i ^ (16 * (k // 2) + 2 * (k % 2))) for i in range(128)])
        for k in range(1, 4)
    ]
    part = (sum(item.astype(f32) for item in parts) * one_after(back)).astype(bf16)
    copies = jnp.broadcast_to(part[None], (64,) + part.shape)
    same_core = [[i * 2 + c for i in range(64)] for c in range(2)]
    own = lax.all_to_all(copies, both, 0, 0, axis_index_groups=same_core, tiled=True)
    grad_query, grad_key, grad_value = unpack(back)
    own = once(own, grad_query).reshape(8, 8 * CROWS, BLK)
    swapped = lax.ppermute(own, "dp", cores)
    grad_weight = finish(scalar(1 - core), swapped, finish(scalar(core), own))
    grad_weight = grad_weight.reshape(out_weight.shape)
    return (grad_query[None], grad_key[None], grad_value[None], grad_weight)


def solution(mesh):
    return jax.shard_map(
        per_device,
        mesh=mesh,
        in_specs=(
            P("dp", "grp", None),
            P("dp", "grp", None),
            P("dp", "grp", None),
            P("dp", "grp", None),
            P(),
            P("dp", None),
        ),
        out_specs=(P("dp", "grp", None), P("dp", "grp", None), P("dp", "grp", None), P()),
        check_vma=False,
    )
```

```python
import functools
import math

import jax
import jax.numpy as jnp
from jax import lax
from jax.experimental import pallas as pl
from jax.experimental.pallas import tpu as pltpu
from jax.sharding import PartitionSpec as P

HEADS = 16
BLK = 128
DH = 80
PAIR = 2 * DH
BIG = 12
GBLOCKS = 16
REST = GBLOCKS - BIG
BIG_CHUNK = 768
CHUNK = 512
SCALE = 1.0 / math.sqrt(DH)
LOG2E = 1.4426950408889634
WEIGHT_SCALE = 1.0 / math.sqrt(16 * GBLOCKS * BLK)
bf16 = jnp.bfloat16
f32 = jnp.float32


def nn(left, right):
    return lax.dot_general(left, right, (((1,), (0,)), ((), ())), preferred_element_type=f32)


def nt(left, right):
    return lax.dot_general(left, right, (((1,), (1,)), ((), ())), preferred_element_type=f32)


def whole(shape):
    return pl.BlockSpec(shape, lambda i: (0,) * len(shape))


def first_big(ids_ref):
    middle = ids_ref[0, GBLOCKS // 2]
    start = jnp.int32(0)
    for i in range(REST):
        start = start + (ids_ref[0, i] < middle).astype(jnp.int32)
    return start


def three_terms(row):
    high = row.astype(bf16).astype(f32)
    middle = (row - high).astype(bf16).astype(f32)
    low = row - high - middle
    zeros = jnp.zeros((BLK - DH - 3, row.shape[1]), f32)
    return jnp.concatenate([high, middle, low, zeros], axis=0).astype(bf16)


def place_of(start, slot):
    if slot < BIG:
        return start + slot
    other = slot - BIG
    return jnp.where(other < start, other, slot)


def columns_of(slot):
    return slice(slot * BLK, (slot + 1) * BLK)


def pack_kernel(copies, weight_ref, grads_ref, query_ref, key_ref, value_ref, *refs):
    out_ref, *half_refs = refs[-1 - copies :]
    arrays = [
        query_ref[...].T,
        key_ref[...].T,
        value_ref[...].T,
        nt(weight_ref[...], grads_ref[...]).astype(bf16),
    ]
    for dest in range(out_ref.shape[0]):
        for block in range(2):
            for which, array in enumerate(arrays):
                out_ref[dest, block, which] = array[
                    dest * DH : (dest + 1) * DH, columns_of(block)
                ]
    for i, half_ref in enumerate(half_refs):
        half_ref[...] = grads_ref[columns_of(i), :]


def pack(half, copies, weight, grads, query, key, value, *after):
    rows, width = query.shape
    column = pl.BlockSpec((rows, width // 2), lambda i: (0, half))
    shapes = [jax.ShapeDtypeStruct((8, 2, 4, DH, BLK), bf16)]
    shapes += [jax.ShapeDtypeStruct((BLK, grads.shape[1]), bf16)] * copies
    return pl.pallas_call(
        functools.partial(pack_kernel, copies),
        grid=(1,),
        in_specs=[
            pl.BlockSpec((width // 2, width), lambda i: (half, 0)),
            whole(grads.shape),
            column,
            column,
            column,
        ]
        + [pl.BlockSpec(memory_space=pltpu.HBM)] * len(after),
        out_specs=[whole(shape.shape) for shape in shapes],
        out_shape=shapes,
        compiler_params=pltpu.CompilerParams(vmem_limit_bytes=65408 * 2**10),
        cost_estimate=pl.CostEstimate(
            flops=rows * width * width, bytes_accessed=5 * 2**20, transcendentals=0
        ),
        name="pack_heads",
    )(weight, grads, query, key, value, *after)


def attention_kernel(ids_ref, me_ref, in_ref, *refs):
    keep_ref, send_ref, out_ref, rows_ref, kv_ref, acc_ref, mixed_ref = refs[-7:]
    start = first_big(ids_ref)
    width = BLK * GBLOCKS
    ones = (lax.broadcasted_iota(jnp.int32, (BLK - DH, width), 0) < 3).astype(bf16)
    zeros = jnp.zeros((BLK - DH, width), bf16)
    for which in range(4):
        rows_ref[which, DH:, :] = ones if which == 2 else zeros
    for slot in range(GBLOCKS):
        block = place_of(start, slot)
        for which in range(4):
            rows_ref[which, :DH, columns_of(slot)] = in_ref[block, which]
    kv_ref[0] = rows_ref[1].T
    kv_ref[1] = rows_ref[2].T
    acc_ref[1:] = jnp.zeros((2, DH, width), f32)

    def chunk(queries, span, bias):
        query_t = rows_ref[0, :, queries]
        scores = nn(kv_ref[0, span, :], query_t)
        if bias is not None:
            scores = scores + bias
        top = jnp.max(scores, axis=0, keepdims=True)
        weights = jnp.exp2((scores - top) * (SCALE * LOG2E))
        weights_low = weights.astype(bf16)
        mixed = nn(rows_ref[2, : DH + 16, span], weights_low)
        inverse = 1.0 / mixed[DH : DH + 1]
        attended = (mixed[:DH] * inverse).astype(bf16)
        mixed_ref[:, queries] = attended
        grads = (rows_ref[3, :DH, queries].astype(f32) * inverse).astype(bf16)
        delta = -jnp.sum(grads.astype(f32) * attended.astype(f32), axis=0, keepdims=True)
        grads_more = jnp.concatenate([grads, three_terms(delta)], axis=0)
        dscores = (weights * nn(kv_ref[1, span, :], grads_more)).astype(bf16)
        acc_ref[0, :, queries] = nn(rows_ref[1, :DH, span], dscores)
        acc_ref[1, :, span] += nt(query_t[:DH], dscores)
        acc_ref[2, :, span] += nt(grads, weights_low)

    def big_chunk(i, carry):
        chunk(pl.ds(pl.multiple_of(i * BIG_CHUNK, BIG_CHUNK), BIG_CHUNK), slice(0, BIG * BLK), None)
        return carry

    lax.fori_loop(0, BIG * BLK // BIG_CHUNK, big_chunk, 0, unroll=2)

    numbers = [ids_ref[0, place_of(start, BIG + i)] for i in range(REST)]
    for part in range(REST * BLK // CHUNK):
        first = part * (CHUNK // BLK)
        columns = []
        for q in range(first, first + CHUNK // BLK):
            rows = [
                jnp.full((BLK, BLK), jnp.where(numbers[q] == numbers[k], 0.0, -1e30), f32)
                for k in range(REST)
            ]
            columns.append(jnp.concatenate(rows, axis=0))
        queries = slice(BIG * BLK + part * CHUNK, BIG * BLK + (part + 1) * CHUNK)
        chunk(queries, slice(BIG * BLK, GBLOCKS * BLK), jnp.concatenate(columns, axis=1))

    for slot in range(GBLOCKS):
        block = place_of(start, slot)
        own = lax.rem(lax.div(block, 2), 2) == lax.rem(me_ref[0], 2)
        column = lax.div(block, 4) * 2 + lax.rem(block, 2)
        target = pl.ds(pl.multiple_of(column * BLK, BLK), BLK)

        @pl.when(own)
        def _():
            keep_ref[:, target] = mixed_ref[:, columns_of(slot)]

        @pl.when(jnp.logical_not(own))
        def _():
            send_ref[:, target] = mixed_ref[:, columns_of(slot)]

    for slot in range(GBLOCKS):
        block = place_of(start, slot)
        for which in range(3):
            part = acc_ref[which, :, columns_of(slot)]
            if which < 2:
                part = part * SCALE
            out_ref[block, which] = part.astype(bf16)


def attention(head, ids, me, packed, *before):
    tokens = GBLOCKS * BLK
    shapes = [jax.ShapeDtypeStruct((DH, tokens // 2), bf16)] * 2
    shapes += [jax.ShapeDtypeStruct((GBLOCKS, 3, PAIR, BLK), bf16)]
    smem = pl.BlockSpec(memory_space=pltpu.SMEM)
    blocks = [whole(shapes[0].shape)] * 2
    blocks += [pl.BlockSpec((GBLOCKS, 3, DH, BLK), lambda i: (0, 0, head, 0))]
    return pl.pallas_call(
        attention_kernel,
        grid=(1,),
        in_specs=[smem, smem, whole(packed.shape)]
        + [pl.BlockSpec(memory_space=pltpu.HBM)] * len(before),
        out_specs=blocks,
        out_shape=shapes,
        input_output_aliases={3: 2} if before else {},
        scratch_shapes=[
            pltpu.VMEM((4, BLK, tokens), bf16),
            pltpu.VMEM((2, tokens, BLK), bf16),
            pltpu.VMEM((3, DH, tokens), f32),
            pltpu.VMEM((DH, tokens), bf16),
        ],
        compiler_params=pltpu.CompilerParams(vmem_limit_bytes=65408 * 2**10),
        cost_estimate=pl.CostEstimate(
            flops=2 * 6 * 3 * 160 * BLK * BLK * BLK,
            bytes_accessed=4 * 2**20,
            transcendentals=160 * BLK * BLK,
        ),
        name="attention_grads",
    )(ids, me, packed, *before)


def unpack_kernel(in_ref, *out_refs):
    for which, out_ref in enumerate(out_refs):
        for half in range(2):
            rows = [
                in_ref[source, half, which, head * DH : (head + 1) * DH, :]
                for head in range(2)
                for source in range(8)
            ]
            out_ref[half * BLK : (half + 1) * BLK, :] = jnp.concatenate(rows, axis=0).T


def unpack(received):
    count = received.shape[2]
    width = 8 * PAIR
    return pl.pallas_call(
        unpack_kernel,
        out_shape=[jax.ShapeDtypeStruct((2 * BLK, width), bf16)] * count,
        compiler_params=pltpu.CompilerParams(vmem_limit_bytes=24 * 2**20),
        cost_estimate=pl.CostEstimate(flops=0, bytes_accessed=4 * 2**20, transcendentals=0),
        name="unpack_heads",
    )(received)


CROWS = 112


def weight_kernel(me_ref, column_ref, *refs):
    grads_refs, out_refs, both_ref, ring_ref, rows_ref = refs[4:-5], refs[-5:-3], *refs[-3:-1], refs[-1]
    core = lax.rem(column_ref[0], 2)
    low = lax.rem(lax.div(column_ref[0], 2), 2)
    z = lax.div(column_ref[0], 4)
    for i in range(4):
        both_ref[i * DH : (i + 1) * DH] = refs[i][...]
    gx = lax.div(me_ref[0], 2)
    offset = gx * (2 * BLK)
    first = 0
    for grads_ref in grads_refs:
        rows = grads_ref.shape[0]
        columns = pl.ds(pl.multiple_of(lax.rem(offset, both_ref.shape[1]), BLK), rows)
        ring_ref[:, first : first + rows] = both_ref[:, columns]
        offset = offset + rows
        first = first + rows
    left = ring_ref[...]
    width = grads_refs[0].shape[1]
    blocks = []
    for j in range(0, width, 2 * BLK):
        right = jnp.concatenate([ref[:, j : j + 2 * BLK] for ref in grads_refs], axis=0)
        blocks.append(nn(left, right).astype(bf16))
    product = jnp.concatenate(blocks, axis=1)
    per_core = product.shape[1] // BLK // 2
    for which in range(2):
        for half in range(2):
            for j in range(per_core):
                rows_ref[j * PAIR : (j + 1) * PAIR, :] = product[
                    which * PAIR : (which + 1) * PAIR, columns_of(half * per_core + j)
                ]
            rows_ref[per_core * PAIR :, :] = jnp.zeros((8 * CROWS - per_core * PAIR, BLK), bf16)

            def store(out_ref):
                for j in range(8):
                    along_z = lax.bitwise_xor(z, j // 2)
                    along_y = which * 2 + lax.bitwise_xor(low, j % 2)
                    out_ref[along_z, along_y] = rows_ref[j * CROWS : (j + 1) * CROWS, :]

            pl.when(core == half)(lambda: store(out_refs[0]))
            pl.when(core != half)(lambda: store(out_refs[1]))


def weight_terms(me, column, atts, grads):
    vmem = pl.BlockSpec(memory_space=pltpu.VMEM)
    return pl.pallas_call(
        weight_kernel,
        in_specs=[pl.BlockSpec(memory_space=pltpu.SMEM)] * 2 + [vmem] * (4 + len(grads)),
        out_specs=[vmem] * 2,
        out_shape=[jax.ShapeDtypeStruct((4, 4, CROWS, BLK), bf16)] * 2,
        scratch_shapes=[
            pltpu.VMEM((2 * PAIR, atts[0].shape[1]), bf16),
            pltpu.VMEM((2 * PAIR, atts[0].shape[1]), bf16),
            pltpu.VMEM((8 * CROWS, BLK), bf16),
        ],
        compiler_params=pltpu.CompilerParams(vmem_limit_bytes=65408 * 2**10),
        cost_estimate=pl.CostEstimate(
            flops=2 * 2 * PAIR * 4 * grads[0].size, bytes_accessed=6 * 2**20, transcendentals=0
        ),
        name="weight_terms",
    )(me, column, *atts, *grads)


def nothing_kernel(*refs):
    pass


def once(array, *after):
    anywhere = pl.BlockSpec(memory_space=pltpu.HBM)
    return pl.pallas_call(
        nothing_kernel,
        in_specs=[anywhere] * (1 + len(after)),
        out_specs=anywhere,
        out_shape=jax.ShapeDtypeStruct(array.shape, array.dtype),
        input_output_aliases={0: 0},
        compiler_params=pltpu.CompilerParams(vmem_limit_bytes=65408 * 2**10),
        cost_estimate=pl.CostEstimate(flops=0, bytes_accessed=0, transcendentals=0),
        name="once",
    )(array, *after)


def one_kernel(*refs):
    refs[-1][0, 0] = 1.0


def one_after(*after):
    return pl.pallas_call(
        one_kernel,
        in_specs=[pl.BlockSpec(memory_space=pltpu.HBM)] * len(after),
        out_specs=pl.BlockSpec(memory_space=pltpu.SMEM),
        out_shape=jax.ShapeDtypeStruct((1, 1), f32),
        cost_estimate=pl.CostEstimate(flops=0, bytes_accessed=0, transcendentals=0),
        name="one_after",
    )(*after)


def finish_kernel(core_ref, in_ref, *refs):
    out_ref = refs[-1]
    for pair in range(in_ref.shape[0]):
        for j in range(out_ref.shape[3] // BLK):
            block = in_ref[pair, j * PAIR : (j + 1) * PAIR, :].astype(f32) * WEIGHT_SCALE
            for head in range(2):
                out_ref[head, pair, :, columns_of(j)] = block[head * DH : (head + 1) * DH]


def finish(core, rows, *before):
    width = 8 * PAIR
    return pl.pallas_call(
        finish_kernel,
        grid_spec=pltpu.PrefetchScalarGridSpec(
            num_scalar_prefetch=1,
            grid=(2,),
            in_specs=[pl.BlockSpec((4, 8 * CROWS, BLK), lambda i, core: (i, 0, 0))]
            + [pl.BlockSpec(memory_space=pltpu.HBM)] * len(before),
            out_specs=pl.BlockSpec((2, 4, DH, width // 2), lambda i, core: (0, i, 0, core[0])),
        ),
        out_shape=jax.ShapeDtypeStruct((2, 8, DH, width), f32),
        input_output_aliases={2: 0} if before else {},
        compiler_params=pltpu.CompilerParams(vmem_limit_bytes=16 * 2**20),
        cost_estimate=pl.CostEstimate(flops=0, bytes_accessed=5 * 2**20, transcendentals=0),
        name="finish_weight",
    )(core, rows, *before)


def scalar(value):
    return value.astype(jnp.int32).reshape(1)


def per_device(queries, keys_in, value_rows, grad_out, out_weight, image_ids):
    grads_own = grad_out[0]
    both = ("grp", "dp")
    me = scalar(lax.axis_index("grp"))
    core = lax.axis_index("dp") % 2
    operands = (out_weight, grads_own, queries[0], keys_in[0], value_rows[0])
    (packed_first,) = pack(0, 0, *operands)
    packed_second, *grads_late = pack(1, 2, *operands, packed_first)
    shape = (GBLOCKS, 4, DH, BLK)
    first = lax.all_to_all(packed_first, "grp", 0, 0, tiled=True).reshape(shape)
    packed_second = once(packed_second, first)
    second = lax.all_to_all(packed_second, "grp", 0, 0, tiled=True).reshape(shape)
    keep_first, send_first, out = attention(0, image_ids, me, first)
    up = [(i, (i + 2) % 8) for i in range(8)]
    down = [(i, (i + 6) % 8) for i in range(8)]
    grads_late = [once(half, send_first) for half in grads_late]
    grads_left = [lax.ppermute(half, "grp", up) for half in grads_late]
    grads_right = [lax.ppermute(half, "grp", down) for half in grads_late]
    keep, send, out = attention(1, image_ids, me, second, out)
    side = [(i, i ^ 1) for i in range(8)]
    other_first = lax.ppermute(send_first, "grp", side)
    grads_right[0] = once(grads_right[0], send)
    grads_left[1] = once(grads_left[1], send)
    grads_far = [lax.ppermute(grads_right[0], "grp", down), lax.ppermute(grads_left[1], "grp", up)]
    send = once(send, *grads_left, *grads_right)
    send = once(send, other_first)
    other = lax.ppermute(send, "grp", side)
    out = once(out, other, *grads_far)
    back = lax.all_to_all(out.reshape(8, 2, 3, PAIR, BLK), "grp", 0, 0, tiled=True)
    grads_line = (grads_own, *grads_right, *grads_far, *grads_left)
    column = scalar(lax.axis_index("dp"))
    kept, sent = weight_terms(me, column, (keep_first, keep, other_first, other), grads_line)
    cores = [(i, i ^ 1) for i in range(16)]
    sent = lax.ppermute(sent, "dp", cores)
    parts = [(kept[k].astype(f32) + sent[k].astype(f32)).astype(bf16) for k in range(4)]
    parts = [parts[0]] + [
        lax.ppermute(parts[k], "dp", [(i, i ^ (4 * k)) for i in range(16)]) for k in range(1, 4)
    ]
    parts = [sum(item[k].astype(f32) for item in parts).astype(bf16) for k in range(4)]
    parts = [parts[0]] + [
        lax.ppermute(parts[k], both, [(i, i ^ (16 * (k // 2) + 2 * (k % 2))) for i in range(128)])
        for k in range(1, 4)
    ]
    part = (sum(item.astype(f32) for item in parts) * one_after(back)).astype(bf16)
    copies = jnp.broadcast_to(part[None], (64,) + part.shape)
    same_core = [[i * 2 + c for i in range(64)] for c in range(2)]
    own = lax.all_to_all(copies, both, 0, 0, axis_index_groups=same_core, tiled=True)
    grad_query, grad_key, grad_value = unpack(back)
    own = once(own, grad_query).reshape(8, 8 * CROWS, BLK)
    swapped = lax.ppermute(own, "dp", cores)
    grad_weight = finish(scalar(1 - core), swapped, finish(scalar(core), own))
    grad_weight = grad_weight.reshape(out_weight.shape)
    return (grad_query[None], grad_key[None], grad_value[None], grad_weight)


def solution(mesh):
    return jax.shard_map(
        per_device,
        mesh=mesh,
        in_specs=(
            P("dp", "grp", None),
            P("dp", "grp", None),
            P("dp", "grp", None),
            P("dp", "grp", None),
            P(),
            P("dp", None),
        ),
        out_specs=(P("dp", "grp", None), P("dp", "grp", None), P("dp", "grp", None), P()),
        check_vma=False,
    )
```

```python
import functools
import math

import jax
import jax.numpy as jnp
from jax import lax
from jax.experimental import pallas as pl
from jax.experimental.pallas import tpu as pltpu
from jax.sharding import PartitionSpec as P

HEADS = 16
BLK = 128
DH = 80
PAIR = 2 * DH
BIG = 12
GBLOCKS = 16
REST = GBLOCKS - BIG
BIG_CHUNK = 768
CHUNK = 512
SCALE = 1.0 / math.sqrt(DH)
LOG2E = 1.4426950408889634
WEIGHT_SCALE = 1.0 / math.sqrt(16 * GBLOCKS * BLK)
bf16 = jnp.bfloat16
f32 = jnp.float32


def nn(left, right):
    return lax.dot_general(left, right, (((1,), (0,)), ((), ())), preferred_element_type=f32)


def nt(left, right):
    return lax.dot_general(left, right, (((1,), (1,)), ((), ())), preferred_element_type=f32)


def whole(shape):
    return pl.BlockSpec(shape, lambda i: (0,) * len(shape))


def first_big(ids_ref):
    middle = ids_ref[0, GBLOCKS // 2]
    start = jnp.int32(0)
    for i in range(REST):
        start = start + (ids_ref[0, i] < middle).astype(jnp.int32)
    return start


def three_terms(row):
    high = row.astype(bf16).astype(f32)
    middle = (row - high).astype(bf16).astype(f32)
    low = row - high - middle
    zeros = jnp.zeros((BLK - DH - 3, row.shape[1]), f32)
    return jnp.concatenate([high, middle, low, zeros], axis=0).astype(bf16)


def place_of(start, slot):
    if slot < BIG:
        return start + slot
    other = slot - BIG
    return jnp.where(other < start, other, slot)


def columns_of(slot):
    return slice(slot * BLK, (slot + 1) * BLK)


def pack_kernel(copies, weight_ref, grads_ref, query_ref, key_ref, value_ref, *refs):
    out_ref, *half_refs = refs[-1 - copies :]
    arrays = [
        query_ref[...].T,
        key_ref[...].T,
        value_ref[...].T,
        nt(weight_ref[...], grads_ref[...]).astype(bf16),
    ]
    for dest in range(out_ref.shape[0]):
        for block in range(2):
            for which, array in enumerate(arrays):
                out_ref[dest, block, which] = array[
                    dest * DH : (dest + 1) * DH, columns_of(block)
                ]
    for i, half_ref in enumerate(half_refs):
        half_ref[...] = grads_ref[columns_of(i), :]


def pack(half, copies, weight, grads, query, key, value, *after):
    rows, width = query.shape
    column = pl.BlockSpec((rows, width // 2), lambda i: (0, half))
    shapes = [jax.ShapeDtypeStruct((8, 2, 4, DH, BLK), bf16)]
    shapes += [jax.ShapeDtypeStruct((BLK, grads.shape[1]), bf16)] * copies
    return pl.pallas_call(
        functools.partial(pack_kernel, copies),
        grid=(1,),
        in_specs=[
            pl.BlockSpec((width // 2, width), lambda i: (half, 0)),
            whole(grads.shape),
            column,
            column,
            column,
        ]
        + [pl.BlockSpec(memory_space=pltpu.HBM)] * len(after),
        out_specs=[whole(shape.shape) for shape in shapes],
        out_shape=shapes,
        compiler_params=pltpu.CompilerParams(vmem_limit_bytes=65408 * 2**10),
        cost_estimate=pl.CostEstimate(
            flops=rows * width * width, bytes_accessed=5 * 2**20, transcendentals=0
        ),
        name="pack_heads",
    )(weight, grads, query, key, value, *after)


def attention_kernel(ids_ref, me_ref, in_ref, *refs):
    keep_ref, send_ref, out_ref, rows_ref, kv_ref, acc_ref, mixed_ref = refs[-7:]
    start = first_big(ids_ref)
    width = BLK * GBLOCKS
    ones = (lax.broadcasted_iota(jnp.int32, (BLK - DH, width), 0) < 3).astype(bf16)
    zeros = jnp.zeros((BLK - DH, width), bf16)
    for which in range(4):
        rows_ref[which, DH:, :] = ones if which == 2 else zeros
    for slot in range(GBLOCKS):
        block = place_of(start, slot)
        for which in range(4):
            rows_ref[which, :DH, columns_of(slot)] = in_ref[block, which]
    kv_ref[0] = rows_ref[1].T
    kv_ref[1] = rows_ref[2].T
    acc_ref[1:] = jnp.zeros((2, DH, width), f32)

    def chunk(queries, span, bias):
        query_t = rows_ref[0, :, queries]
        scores = nn(kv_ref[0, span, :], query_t)
        if bias is not None:
            scores = scores + bias
        top = jnp.max(scores, axis=0, keepdims=True)
        weights = jnp.exp2((scores - top) * (SCALE * LOG2E))
        weights_low = weights.astype(bf16)
        mixed = nn(rows_ref[2, : DH + 16, span], weights_low)
        inverse = 1.0 / mixed[DH : DH + 1]
        attended = (mixed[:DH] * inverse).astype(bf16)
        mixed_ref[:, queries] = attended
        grads = (rows_ref[3, :DH, queries].astype(f32) * inverse).astype(bf16)
        delta = -jnp.sum(grads.astype(f32) * attended.astype(f32), axis=0, keepdims=True)
        grads_more = jnp.concatenate([grads, three_terms(delta)], axis=0)
        dscores = (weights * nn(kv_ref[1, span, :], grads_more)).astype(bf16)
        acc_ref[0, :, queries] = nn(rows_ref[1, :DH, span], dscores)
        acc_ref[1, :, span] += nt(query_t[:DH], dscores)
        acc_ref[2, :, span] += nt(grads, weights_low)

    def big_chunk(i, carry):
        chunk(pl.ds(pl.multiple_of(i * BIG_CHUNK, BIG_CHUNK), BIG_CHUNK), slice(0, BIG * BLK), None)
        return carry

    lax.fori_loop(0, BIG * BLK // BIG_CHUNK, big_chunk, 0, unroll=2)

    numbers = [ids_ref[0, place_of(start, BIG + i)] for i in range(REST)]
    for part in range(REST * BLK // CHUNK):
        first = part * (CHUNK // BLK)
        columns = []
        for q in range(first, first + CHUNK // BLK):
            rows = [
                jnp.full((BLK, BLK), jnp.where(numbers[q] == numbers[k], 0.0, -1e30), f32)
                for k in range(REST)
            ]
            columns.append(jnp.concatenate(rows, axis=0))
        queries = slice(BIG * BLK + part * CHUNK, BIG * BLK + (part + 1) * CHUNK)
        chunk(queries, slice(BIG * BLK, GBLOCKS * BLK), jnp.concatenate(columns, axis=1))

    for slot in range(GBLOCKS):
        block = place_of(start, slot)
        own = lax.rem(lax.div(block, 2), 2) == lax.rem(me_ref[0], 2)
        column = lax.div(block, 4) * 2 + lax.rem(block, 2)
        target = pl.ds(pl.multiple_of(column * BLK, BLK), BLK)

        @pl.when(own)
        def _():
            keep_ref[:, target] = mixed_ref[:, columns_of(slot)]

        @pl.when(jnp.logical_not(own))
        def _():
            send_ref[:, target] = mixed_ref[:, columns_of(slot)]

    for slot in range(GBLOCKS):
        block = place_of(start, slot)
        for which in range(3):
            part = acc_ref[which, :, columns_of(slot)]
            if which < 2:
                part = part * SCALE
            out_ref[block, which] = part.astype(bf16)


def attention(head, ids, me, packed, *before):
    tokens = GBLOCKS * BLK
    shapes = [jax.ShapeDtypeStruct((DH, tokens // 2), bf16)] * 2
    shapes += [jax.ShapeDtypeStruct((GBLOCKS, 3, PAIR, BLK), bf16)]
    smem = pl.BlockSpec(memory_space=pltpu.SMEM)
    blocks = [whole(shapes[0].shape)] * 2
    blocks += [pl.BlockSpec((GBLOCKS, 3, DH, BLK), lambda i: (0, 0, head, 0))]
    return pl.pallas_call(
        attention_kernel,
        grid=(1,),
        in_specs=[smem, smem, whole(packed.shape)]
        + [pl.BlockSpec(memory_space=pltpu.HBM)] * len(before),
        out_specs=blocks,
        out_shape=shapes,
        input_output_aliases={3: 2} if before else {},
        scratch_shapes=[
            pltpu.VMEM((4, BLK, tokens), bf16),
            pltpu.VMEM((2, tokens, BLK), bf16),
            pltpu.VMEM((3, DH, tokens), f32),
            pltpu.VMEM((DH, tokens), bf16),
        ],
        compiler_params=pltpu.CompilerParams(vmem_limit_bytes=65408 * 2**10),
        cost_estimate=pl.CostEstimate(
            flops=2 * 6 * 3 * 160 * BLK * BLK * BLK,
            bytes_accessed=4 * 2**20,
            transcendentals=160 * BLK * BLK,
        ),
        name="attention_grads",
    )(ids, me, packed, *before)


def unpack_kernel(in_ref, *out_refs):
    for which, out_ref in enumerate(out_refs):
        for half in range(2):
            rows = [
                in_ref[source, half, which, head * DH : (head + 1) * DH, :]
                for head in range(2)
                for source in range(8)
            ]
            out_ref[half * BLK : (half + 1) * BLK, :] = jnp.concatenate(rows, axis=0).T


def unpack(received):
    count = received.shape[2]
    width = 8 * PAIR
    return pl.pallas_call(
        unpack_kernel,
        out_shape=[jax.ShapeDtypeStruct((2 * BLK, width), bf16)] * count,
        compiler_params=pltpu.CompilerParams(vmem_limit_bytes=24 * 2**20),
        cost_estimate=pl.CostEstimate(flops=0, bytes_accessed=4 * 2**20, transcendentals=0),
        name="unpack_heads",
    )(received)


CROWS = 104


def weight_kernel(me_ref, column_ref, *refs):
    grads_refs, out_refs, both_ref, ring_ref, rows_ref = refs[4:-5], refs[-5:-3], *refs[-3:-1], refs[-1]
    core = lax.rem(column_ref[0], 2)
    low = lax.rem(lax.div(column_ref[0], 2), 2)
    z = lax.div(column_ref[0], 4)
    for i in range(4):
        both_ref[i * DH : (i + 1) * DH] = refs[i][...]
    gx = lax.div(me_ref[0], 2)
    offset = gx * (2 * BLK)
    first = 0
    for grads_ref in grads_refs:
        rows = grads_ref.shape[0]
        columns = pl.ds(pl.multiple_of(lax.rem(offset, both_ref.shape[1]), BLK), rows)
        ring_ref[:, first : first + rows] = both_ref[:, columns]
        offset = offset + rows
        first = first + rows
    left = ring_ref[...]
    width = grads_refs[0].shape[1]
    blocks = []
    for j in range(0, width, 2 * BLK):
        right = jnp.concatenate([ref[:, j : j + 2 * BLK] for ref in grads_refs], axis=0)
        blocks.append(nn(left, right))
    product = jnp.concatenate(blocks, axis=1)
    per_core = product.shape[1] // BLK // 2
    for which in range(2):
        for half in range(2):
            for j in range(per_core):
                rows_ref[j * PAIR : (j + 1) * PAIR, :] = product[
                    which * PAIR : (which + 1) * PAIR, columns_of(half * per_core + j)
                ]
            rows_ref[per_core * PAIR :, :] = jnp.zeros((8 * CROWS - per_core * PAIR, BLK), f32)

            def store(out_ref):
                for j in range(8):
                    along_z = lax.bitwise_xor(z, j // 2)
                    along_y = which * 2 + lax.bitwise_xor(low, j % 2)
                    chunk = rows_ref[j * CROWS : (j + 1) * CROWS, :]
                    out_ref[along_z, along_y] = chunk.astype(bf16)

            pl.when(core == half)(lambda: store(out_refs[0]))
            pl.when(core != half)(lambda: store(out_refs[1]))


def weight_terms(me, column, atts, grads):
    vmem = pl.BlockSpec(memory_space=pltpu.VMEM)
    return pl.pallas_call(
        weight_kernel,
        in_specs=[pl.BlockSpec(memory_space=pltpu.SMEM)] * 2 + [vmem] * (4 + len(grads)),
        out_specs=[vmem] * 2,
        out_shape=[jax.ShapeDtypeStruct((4, 4, CROWS, BLK), bf16)] * 2,
        scratch_shapes=[
            pltpu.VMEM((2 * PAIR, atts[0].shape[1]), bf16),
            pltpu.VMEM((2 * PAIR, atts[0].shape[1]), bf16),
            pltpu.VMEM((8 * CROWS, BLK), f32),
        ],
        compiler_params=pltpu.CompilerParams(vmem_limit_bytes=65408 * 2**10),
        cost_estimate=pl.CostEstimate(
            flops=2 * 2 * PAIR * 4 * grads[0].size, bytes_accessed=6 * 2**20, transcendentals=0
        ),
        name="weight_terms",
    )(me, column, *atts, *grads)


def nothing_kernel(*refs):
    pass


def once(array, *after):
    anywhere = pl.BlockSpec(memory_space=pltpu.HBM)
    return pl.pallas_call(
        nothing_kernel,
        in_specs=[anywhere] * (1 + len(after)),
        out_specs=anywhere,
        out_shape=jax.ShapeDtypeStruct(array.shape, array.dtype),
        input_output_aliases={0: 0},
        compiler_params=pltpu.CompilerParams(vmem_limit_bytes=65408 * 2**10),
        cost_estimate=pl.CostEstimate(flops=0, bytes_accessed=0, transcendentals=0),
        name="once",
    )(array, *after)


def one_kernel(*refs):
    refs[-1][0, 0] = 1.0


def one_after(*after):
    return pl.pallas_call(
        one_kernel,
        in_specs=[pl.BlockSpec(memory_space=pltpu.HBM)] * len(after),
        out_specs=pl.BlockSpec(memory_space=pltpu.SMEM),
        out_shape=jax.ShapeDtypeStruct((1, 1), f32),
        cost_estimate=pl.CostEstimate(flops=0, bytes_accessed=0, transcendentals=0),
        name="one_after",
    )(*after)


def finish_kernel(core_ref, in_ref, *refs):
    out_ref = refs[-1]
    for pair in range(in_ref.shape[0]):
        for j in range(out_ref.shape[3] // BLK):
            block = in_ref[pair, j * PAIR : (j + 1) * PAIR, :].astype(f32) * WEIGHT_SCALE
            for head in range(2):
                out_ref[head, pair, :, columns_of(j)] = block[head * DH : (head + 1) * DH]


def finish(core, rows, *before):
    width = 8 * PAIR
    return pl.pallas_call(
        finish_kernel,
        grid_spec=pltpu.PrefetchScalarGridSpec(
            num_scalar_prefetch=1,
            grid=(2,),
            in_specs=[pl.BlockSpec((4, 8 * CROWS, BLK), lambda i, core: (i, 0, 0))]
            + [pl.BlockSpec(memory_space=pltpu.HBM)] * len(before),
            out_specs=pl.BlockSpec((2, 4, DH, width // 2), lambda i, core: (0, i, 0, core[0])),
        ),
        out_shape=jax.ShapeDtypeStruct((2, 8, DH, width), f32),
        input_output_aliases={2: 0} if before else {},
        compiler_params=pltpu.CompilerParams(vmem_limit_bytes=16 * 2**20),
        cost_estimate=pl.CostEstimate(flops=0, bytes_accessed=5 * 2**20, transcendentals=0),
        name="finish_weight",
    )(core, rows, *before)


def scalar(value):
    return value.astype(jnp.int32).reshape(1)


def per_device(queries, keys_in, value_rows, grad_out, out_weight, image_ids):
    grads_own = grad_out[0]
    both = ("grp", "dp")
    me = scalar(lax.axis_index("grp"))
    core = lax.axis_index("dp") % 2
    operands = (out_weight, grads_own, queries[0], keys_in[0], value_rows[0])
    (packed_first,) = pack(0, 0, *operands)
    packed_second, *grads_late = pack(1, 2, *operands, packed_first)
    shape = (GBLOCKS, 4, DH, BLK)
    first = lax.all_to_all(packed_first, "grp", 0, 0, tiled=True).reshape(shape)
    packed_second = once(packed_second, first)
    second = lax.all_to_all(packed_second, "grp", 0, 0, tiled=True).reshape(shape)
    keep_first, send_first, out = attention(0, image_ids, me, first)
    up = [(i, (i + 2) % 8) for i in range(8)]
    down = [(i, (i + 6) % 8) for i in range(8)]
    grads_late = [once(half, send_first) for half in grads_late]
    grads_left = [lax.ppermute(half, "grp", up) for half in grads_late]
    grads_right = [lax.ppermute(half, "grp", down) for half in grads_late]
    keep, send, out = attention(1, image_ids, me, second, out)
    side = [(i, i ^ 1) for i in range(8)]
    other_first = lax.ppermute(send_first, "grp", side)
    grads_right[0] = once(grads_right[0], send)
    grads_left[1] = once(grads_left[1], send)
    grads_far = [lax.ppermute(grads_right[0], "grp", down), lax.ppermute(grads_left[1], "grp", up)]
    send = once(send, *grads_left, *grads_right)
    send = once(send, other_first)
    other = lax.ppermute(send, "grp", side)
    out = once(out, other, *grads_far)
    back = lax.all_to_all(out.reshape(8, 2, 3, PAIR, BLK), "grp", 0, 0, tiled=True)
    grads_line = (grads_own, *grads_right, *grads_far, *grads_left)
    column = scalar(lax.axis_index("dp"))
    kept, sent = weight_terms(me, column, (keep_first, keep, other_first, other), grads_line)
    cores = [(i, i ^ 1) for i in range(16)]
    sent = lax.ppermute(sent, "dp", cores)
    parts = [(kept[k].astype(f32) + sent[k].astype(f32)).astype(bf16) for k in range(4)]
    parts = [parts[0]] + [
        lax.ppermute(parts[k], "dp", [(i, i ^ (4 * k)) for i in range(16)]) for k in range(1, 4)
    ]
    parts = [sum(item[k].astype(f32) for item in parts).astype(bf16) for k in range(4)]
    parts = [parts[0]] + [
        lax.ppermute(parts[k], both, [(i, i ^ (16 * (k // 2) + 2 * (k % 2))) for i in range(128)])
        for k in range(1, 4)
    ]
    part = (sum(item.astype(f32) for item in parts) * one_after(back)).astype(bf16)
    copies = jnp.broadcast_to(part[None], (64,) + part.shape)
    same_core = [[i * 2 + c for i in range(64)] for c in range(2)]
    own = lax.all_to_all(copies, both, 0, 0, axis_index_groups=same_core, tiled=True)
    grad_query, grad_key, grad_value = unpack(back)
    own = once(own, grad_query).reshape(8, 8 * CROWS, BLK)
    swapped = lax.ppermute(own, "dp", cores)
    grad_weight = finish(scalar(1 - core), swapped, finish(scalar(core), own))
    grad_weight = grad_weight.reshape(out_weight.shape)
    return (grad_query[None], grad_key[None], grad_value[None], grad_weight)


def solution(mesh):
    return jax.shard_map(
        per_device,
        mesh=mesh,
        in_specs=(
            P("dp", "grp", None),
            P("dp", "grp", None),
            P("dp", "grp", None),
            P("dp", "grp", None),
            P(),
            P("dp", None),
        ),
        out_specs=(P("dp", "grp", None), P("dp", "grp", None), P("dp", "grp", None), P()),
        check_vma=False,
    )
```

```python
import functools
import math

import jax
import jax.numpy as jnp
from jax import lax
from jax.experimental import pallas as pl
from jax.experimental.pallas import tpu as pltpu
from jax.sharding import PartitionSpec as P

HEADS = 16
BLK = 128
DH = 80
PAIR = 2 * DH
BIG = 12
GBLOCKS = 16
REST = GBLOCKS - BIG
BIG_CHUNK = 768
CHUNK = 512
SCALE = 1.0 / math.sqrt(DH)
LOG2E = 1.4426950408889634
WEIGHT_SCALE = 1.0 / math.sqrt(16 * GBLOCKS * BLK)
bf16 = jnp.bfloat16
f32 = jnp.float32


def nn(left, right):
    return lax.dot_general(left, right, (((1,), (0,)), ((), ())), preferred_element_type=f32)


def nt(left, right):
    return lax.dot_general(left, right, (((1,), (1,)), ((), ())), preferred_element_type=f32)


def whole(shape):
    return pl.BlockSpec(shape, lambda i: (0,) * len(shape))


def first_big(ids_ref):
    middle = ids_ref[0, GBLOCKS // 2]
    start = jnp.int32(0)
    for i in range(REST):
        start = start + (ids_ref[0, i] < middle).astype(jnp.int32)
    return start


def three_terms(row):
    high = row.astype(bf16).astype(f32)
    middle = (row - high).astype(bf16).astype(f32)
    low = row - high - middle
    zeros = jnp.zeros((BLK - DH - 3, row.shape[1]), f32)
    return jnp.concatenate([high, middle, low, zeros], axis=0).astype(bf16)


def place_of(start, slot):
    if slot < BIG:
        return start + slot
    other = slot - BIG
    return jnp.where(other < start, other, slot)


def columns_of(slot):
    return slice(slot * BLK, (slot + 1) * BLK)


def pack_kernel(copies, weight_ref, grads_ref, query_ref, key_ref, value_ref, *refs):
    out_ref, *half_refs = refs[-1 - copies :]
    arrays = [
        query_ref[...].T,
        key_ref[...].T,
        value_ref[...].T,
        nt(weight_ref[...], grads_ref[...]).astype(bf16),
    ]
    for dest in range(out_ref.shape[0]):
        for block in range(2):
            for which, array in enumerate(arrays):
                out_ref[dest, block, which] = array[
                    dest * DH : (dest + 1) * DH, columns_of(block)
                ]
    for i, half_ref in enumerate(half_refs):
        half_ref[...] = grads_ref[columns_of(i), :]


def pack(half, copies, weight, grads, query, key, value, *after):
    rows, width = query.shape
    column = pl.BlockSpec((rows, width // 2), lambda i: (0, half))
    shapes = [jax.ShapeDtypeStruct((8, 2, 4, DH, BLK), bf16)]
    shapes += [jax.ShapeDtypeStruct((BLK, grads.shape[1]), bf16)] * copies
    return pl.pallas_call(
        functools.partial(pack_kernel, copies),
        grid=(1,),
        in_specs=[
            pl.BlockSpec((width // 2, width), lambda i: (half, 0)),
            whole(grads.shape),
            column,
            column,
            column,
        ]
        + [pl.BlockSpec(memory_space=pltpu.HBM)] * len(after),
        out_specs=[whole(shape.shape) for shape in shapes],
        out_shape=shapes,
        compiler_params=pltpu.CompilerParams(vmem_limit_bytes=65408 * 2**10),
        cost_estimate=pl.CostEstimate(
            flops=rows * width * width, bytes_accessed=5 * 2**20, transcendentals=0
        ),
        name="pack_heads",
    )(weight, grads, query, key, value, *after)


def attention_kernel(ids_ref, me_ref, in_ref, *refs):
    keep_ref, send_ref, out_ref, rows_ref, kv_ref, acc_ref, mixed_ref = refs[-7:]
    start = first_big(ids_ref)
    width = BLK * GBLOCKS
    ones = (lax.broadcasted_iota(jnp.int32, (BLK - DH, width), 0) < 3).astype(bf16)
    zeros = jnp.zeros((BLK - DH, width), bf16)
    for which in range(4):
        rows_ref[which, DH:, :] = ones if which == 2 else zeros
    for slot in range(GBLOCKS):
        block = place_of(start, slot)
        for which in range(4):
            rows_ref[which, :DH, columns_of(slot)] = in_ref[block, which]
    kv_ref[0] = rows_ref[1].T
    kv_ref[1] = rows_ref[2].T
    acc_ref[1:] = jnp.zeros((2, DH, width), f32)

    def chunk(queries, span, bias):
        query_t = rows_ref[0, :, queries]
        scores = nn(kv_ref[0, span, :], query_t)
        if bias is not None:
            scores = scores + bias
        top = jnp.max(scores, axis=0, keepdims=True)
        weights = jnp.exp2((scores - top) * (SCALE * LOG2E))
        weights_low = weights.astype(bf16)
        mixed = nn(rows_ref[2, : DH + 16, span], weights_low)
        inverse = 1.0 / mixed[DH : DH + 1]
        attended = (mixed[:DH] * inverse).astype(bf16)
        mixed_ref[:, queries] = attended
        grads = (rows_ref[3, :DH, queries].astype(f32) * inverse).astype(bf16)
        delta = -jnp.sum(grads.astype(f32) * attended.astype(f32), axis=0, keepdims=True)
        grads_more = jnp.concatenate([grads, three_terms(delta)], axis=0)
        dscores = (weights * nn(kv_ref[1, span, :], grads_more)).astype(bf16)
        acc_ref[0, :, queries] = nn(rows_ref[1, :DH, span], dscores)
        acc_ref[1, :, span] += nt(query_t[:DH], dscores)
        acc_ref[2, :, span] += nt(grads, weights_low)

    def big_chunk(i, carry):
        chunk(pl.ds(pl.multiple_of(i * BIG_CHUNK, BIG_CHUNK), BIG_CHUNK), slice(0, BIG * BLK), None)
        return carry

    lax.fori_loop(0, BIG * BLK // BIG_CHUNK, big_chunk, 0, unroll=2)

    numbers = [ids_ref[0, place_of(start, BIG + i)] for i in range(REST)]
    for part in range(REST * BLK // CHUNK):
        first = part * (CHUNK // BLK)
        columns = []
        for q in range(first, first + CHUNK // BLK):
            rows = [
                jnp.full((BLK, BLK), jnp.where(numbers[q] == numbers[k], 0.0, -1e30), f32)
                for k in range(REST)
            ]
            columns.append(jnp.concatenate(rows, axis=0))
        queries = slice(BIG * BLK + part * CHUNK, BIG * BLK + (part + 1) * CHUNK)
        chunk(queries, slice(BIG * BLK, GBLOCKS * BLK), jnp.concatenate(columns, axis=1))

    for slot in range(GBLOCKS):
        block = place_of(start, slot)
        own = lax.rem(lax.div(block, 2), 2) == lax.rem(me_ref[0], 2)
        column = lax.div(block, 4) * 2 + lax.rem(block, 2)
        target = pl.ds(pl.multiple_of(column * BLK, BLK), BLK)

        @pl.when(own)
        def _():
            keep_ref[:, target] = mixed_ref[:, columns_of(slot)]

        @pl.when(jnp.logical_not(own))
        def _():
            send_ref[:, target] = mixed_ref[:, columns_of(slot)]

    for slot in range(GBLOCKS):
        block = place_of(start, slot)
        for which in range(3):
            part = acc_ref[which, :, columns_of(slot)]
            if which < 2:
                part = part * SCALE
            out_ref[block, which] = part.astype(bf16)


def attention(head, ids, me, packed, *before):
    tokens = GBLOCKS * BLK
    shapes = [jax.ShapeDtypeStruct((DH, tokens // 2), bf16)] * 2
    shapes += [jax.ShapeDtypeStruct((GBLOCKS, 3, PAIR, BLK), bf16)]
    smem = pl.BlockSpec(memory_space=pltpu.SMEM)
    blocks = [whole(shapes[0].shape)] * 2
    blocks += [pl.BlockSpec((GBLOCKS, 3, DH, BLK), lambda i: (0, 0, head, 0))]
    return pl.pallas_call(
        attention_kernel,
        grid=(1,),
        in_specs=[smem, smem, whole(packed.shape)]
        + [pl.BlockSpec(memory_space=pltpu.HBM)] * len(before),
        out_specs=blocks,
        out_shape=shapes,
        input_output_aliases={3: 2} if before else {},
        scratch_shapes=[
            pltpu.VMEM((4, BLK, tokens), bf16),
            pltpu.VMEM((2, tokens, BLK), bf16),
            pltpu.VMEM((3, DH, tokens), f32),
            pltpu.VMEM((DH, tokens), bf16),
        ],
        compiler_params=pltpu.CompilerParams(vmem_limit_bytes=65408 * 2**10),
        cost_estimate=pl.CostEstimate(
            flops=2 * 6 * 3 * 160 * BLK * BLK * BLK,
            bytes_accessed=4 * 2**20,
            transcendentals=160 * BLK * BLK,
        ),
        name="attention_grads",
    )(ids, me, packed, *before)


def unpack_kernel(in_ref, *out_refs):
    for which, out_ref in enumerate(out_refs):
        for half in range(2):
            rows = [
                in_ref[source, half, which, head * DH : (head + 1) * DH, :]
                for head in range(2)
                for source in range(8)
            ]
            out_ref[half * BLK : (half + 1) * BLK, :] = jnp.concatenate(rows, axis=0).T


def unpack(received):
    count = received.shape[2]
    width = 8 * PAIR
    return pl.pallas_call(
        unpack_kernel,
        out_shape=[jax.ShapeDtypeStruct((2 * BLK, width), bf16)] * count,
        compiler_params=pltpu.CompilerParams(vmem_limit_bytes=24 * 2**20),
        cost_estimate=pl.CostEstimate(flops=0, bytes_accessed=4 * 2**20, transcendentals=0),
        name="unpack_heads",
    )(received)


CROWS = 104


def weight_kernel(me_ref, column_ref, *refs):
    grads_refs, out_refs, both_ref, ring_ref, rows_ref = refs[4:-5], refs[-5:-3], *refs[-3:-1], refs[-1]
    core = lax.rem(column_ref[0], 2)
    low = lax.rem(lax.div(column_ref[0], 2), 2)
    z = lax.div(column_ref[0], 4)
    for i in range(4):
        both_ref[i * DH : (i + 1) * DH] = refs[i][...]
    gx = lax.div(me_ref[0], 2)
    offset = gx * (2 * BLK)
    first = 0
    for grads_ref in grads_refs:
        rows = grads_ref.shape[0]
        columns = pl.ds(pl.multiple_of(lax.rem(offset, both_ref.shape[1]), BLK), rows)
        ring_ref[:, first : first + rows] = both_ref[:, columns]
        offset = offset + rows
        first = first + rows
    left = ring_ref[...]
    width = grads_refs[0].shape[1]
    blocks = []
    for j in range(0, width, 2 * BLK):
        right = jnp.concatenate([ref[:, j : j + 2 * BLK] for ref in grads_refs], axis=0)
        blocks.append(nn(left, right))
    product = jnp.concatenate(blocks, axis=1)
    per_core = product.shape[1] // BLK // 2
    for which in range(2):
        for half in range(2):
            for j in range(per_core):
                rows_ref[j * PAIR : (j + 1) * PAIR, :] = product[
                    which * PAIR : (which + 1) * PAIR, columns_of(half * per_core + j)
                ]
            rows_ref[per_core * PAIR :, :] = jnp.zeros((8 * CROWS - per_core * PAIR, BLK), f32)

            def store(out_ref):
                for j in range(8):
                    along_z = lax.bitwise_xor(z, j // 2)
                    along_y = which * 2 + lax.bitwise_xor(low, j % 2)
                    chunk = rows_ref[j * CROWS : (j + 1) * CROWS, :]
                    out_ref[along_z, along_y] = chunk.astype(bf16)

            pl.when(core == half)(lambda: store(out_refs[0]))
            pl.when(core != half)(lambda: store(out_refs[1]))


def weight_terms(me, column, atts, grads):
    vmem = pl.BlockSpec(memory_space=pltpu.VMEM)
    return pl.pallas_call(
        weight_kernel,
        in_specs=[pl.BlockSpec(memory_space=pltpu.SMEM)] * 2 + [vmem] * (4 + len(grads)),
        out_specs=[vmem] * 2,
        out_shape=[jax.ShapeDtypeStruct((4, 4, CROWS, BLK), bf16)] * 2,
        scratch_shapes=[
            pltpu.VMEM((2 * PAIR, atts[0].shape[1]), bf16),
            pltpu.VMEM((2 * PAIR, atts[0].shape[1]), bf16),
            pltpu.VMEM((8 * CROWS, BLK), f32),
        ],
        compiler_params=pltpu.CompilerParams(vmem_limit_bytes=65408 * 2**10),
        cost_estimate=pl.CostEstimate(
            flops=2 * 2 * PAIR * 4 * grads[0].size, bytes_accessed=6 * 2**20, transcendentals=0
        ),
        name="weight_terms",
    )(me, column, *atts, *grads)


def nothing_kernel(*refs):
    pass


def once(array, *after):
    anywhere = pl.BlockSpec(memory_space=pltpu.HBM)
    return pl.pallas_call(
        nothing_kernel,
        in_specs=[anywhere] * (1 + len(after)),
        out_specs=anywhere,
        out_shape=jax.ShapeDtypeStruct(array.shape, array.dtype),
        input_output_aliases={0: 0},
        compiler_params=pltpu.CompilerParams(vmem_limit_bytes=65408 * 2**10),
        cost_estimate=pl.CostEstimate(flops=0, bytes_accessed=0, transcendentals=0),
        name="once",
    )(array, *after)


def finish_kernel(core_ref, in_ref, *refs):
    out_ref = refs[-1]
    for pair in range(in_ref.shape[0]):
        for j in range(out_ref.shape[3] // BLK):
            block = in_ref[pair, j * PAIR : (j + 1) * PAIR, :].astype(f32) * WEIGHT_SCALE
            for head in range(2):
                out_ref[head, pair, :, columns_of(j)] = block[head * DH : (head + 1) * DH]


def finish(core, rows, *before):
    width = 8 * PAIR
    return pl.pallas_call(
        finish_kernel,
        grid_spec=pltpu.PrefetchScalarGridSpec(
            num_scalar_prefetch=1,
            grid=(2,),
            in_specs=[pl.BlockSpec((4, 8 * CROWS, BLK), lambda i, core: (i, 0, 0))]
            + [pl.BlockSpec(memory_space=pltpu.HBM)] * len(before),
            out_specs=pl.BlockSpec((2, 4, DH, width // 2), lambda i, core: (0, i, 0, core[0])),
        ),
        out_shape=jax.ShapeDtypeStruct((2, 8, DH, width), f32),
        input_output_aliases={2: 0} if before else {},
        compiler_params=pltpu.CompilerParams(vmem_limit_bytes=16 * 2**20),
        cost_estimate=pl.CostEstimate(flops=0, bytes_accessed=5 * 2**20, transcendentals=0),
        name="finish_weight",
    )(core, rows, *before)


def scalar(value):
    return value.astype(jnp.int32).reshape(1)


def per_device(queries, keys_in, value_rows, grad_out, out_weight, image_ids):
    grads_own = grad_out[0]
    both = ("grp", "dp")
    me = scalar(lax.axis_index("grp"))
    core = lax.axis_index("dp") % 2
    operands = (out_weight, grads_own, queries[0], keys_in[0], value_rows[0])
    (packed_first,) = pack(0, 0, *operands)
    packed_second, *grads_late = pack(1, 2, *operands, packed_first)
    shape = (GBLOCKS, 4, DH, BLK)
    first = lax.all_to_all(packed_first, "grp", 0, 0, tiled=True).reshape(shape)
    packed_second = once(packed_second, first)
    second = lax.all_to_all(packed_second, "grp", 0, 0, tiled=True).reshape(shape)
    keep_first, send_first, out = attention(0, image_ids, me, first)
    up = [(i, (i + 2) % 8) for i in range(8)]
    down = [(i, (i + 6) % 8) for i in range(8)]
    grads_late = [once(half, send_first) for half in grads_late]
    grads_left = [lax.ppermute(half, "grp", up) for half in grads_late]
    grads_right = [lax.ppermute(half, "grp", down) for half in grads_late]
    keep, send, out = attention(1, image_ids, me, second, out)
    side = [(i, i ^ 1) for i in range(8)]
    other_first = lax.ppermute(send_first, "grp", side)
    grads_right[0] = once(grads_right[0], send)
    grads_left[1] = once(grads_left[1], send)
    grads_far = [lax.ppermute(grads_right[0], "grp", down), lax.ppermute(grads_left[1], "grp", up)]
    send = once(send, other_first, *grads_left, *grads_right)
    other = lax.ppermute(send, "grp", side)
    out = once(out, other, *grads_far)
    back = lax.all_to_all(out.reshape(8, 2, 3, PAIR, BLK), "grp", 0, 0, tiled=True)
    grads_line = (grads_own, *grads_right, *grads_far, *grads_left)
    column = scalar(lax.axis_index("dp"))
    kept, sent = weight_terms(me, column, (keep_first, keep, other_first, other), grads_line)
    cores = [(i, i ^ 1) for i in range(16)]
    sent = lax.ppermute(sent, "dp", cores)
    parts = [(kept[k].astype(f32) + sent[k].astype(f32)).astype(bf16) for k in range(4)]
    parts = [parts[0]] + [
        lax.ppermute(parts[k], "dp", [(i, i ^ (4 * k)) for i in range(16)]) for k in range(1, 4)
    ]
    parts = [sum(item[k].astype(f32) for item in parts).astype(bf16) for k in range(4)]
    parts = [parts[0]] + [
        lax.ppermute(parts[k], both, [(i, i ^ (16 * (k // 2) + 2 * (k % 2))) for i in range(128)])
        for k in range(1, 4)
    ]
    part = sum(item.astype(f32) for item in parts).astype(bf16)
    copies = jnp.broadcast_to(part[None], (64,) + part.shape)
    same_core = [[i * 2 + c for i in range(64)] for c in range(2)]
    own = lax.all_to_all(copies, both, 0, 0, axis_index_groups=same_core, tiled=True)
    grad_query, grad_key, grad_value = unpack(back)
    own = once(own, grad_query).reshape(8, 8 * CROWS, BLK)
    swapped = lax.ppermute(own, "dp", cores)
    grad_weight = finish(scalar(1 - core), swapped, finish(scalar(core), own))
    grad_weight = grad_weight.reshape(out_weight.shape)
    return (grad_query[None], grad_key[None], grad_value[None], grad_weight)


def solution(mesh):
    return jax.shard_map(
        per_device,
        mesh=mesh,
        in_specs=(
            P("dp", "grp", None),
            P("dp", "grp", None),
            P("dp", "grp", None),
            P("dp", "grp", None),
            P(),
            P("dp", None),
        ),
        out_specs=(P("dp", "grp", None), P("dp", "grp", None), P("dp", "grp", None), P()),
        check_vma=False,
    )
```
